32 devices in a mesh: dp: 4 (over y, core), seq: 8 (over z, x).
Axes of the slice: x: 2, y: 2, z: 4, core: 2. Of those that a mesh axis runs over, the one named last changes fastest.
Arguments:
- queries: bfloat16 [8, 512, 1536], P('dp', 'seq'), may hold values from -6 to 6
- key_rows: bfloat16 [8, 512, 1536], P('dp', 'seq'), may hold values from -6 to 6
- value_rows: bfloat16 [8, 512, 1536], P('dp', 'seq'), may hold values from -6 to 6
- layer_input: bfloat16 [8, 512, 1536], P('dp', 'seq'), may hold values from -6 to 6
- utt_lengths: int32 [8], P('dp'), may hold values from 128 to 512, as said below
- out_weight: bfloat16 [1536, 1536], replicated, may hold values from -0.15625 to 0.15625
- conv_kernel: bfloat16 [31, 1536], replicated, may hold values from -1 to 1
- conv_cotangent: bfloat16 [8, 512, 1536], P('dp', 'seq'), may hold values from -6 to 6
- pick_weight: int32 [23592], replicated, may hold values from 0 to 2359295
- pick_kernel: int32 [476], replicated, may hold values from 0 to 47615
Outputs:
- conv_out: bfloat16 [8, 512, 1536], P('dp', 'seq')
- context_grad: bfloat16 [8, 512, 1536], P('dp', 'seq')
- weight_picks: float32 [23592], replicated
- kernel_picks: float32 [476], replicated
The draws below stay inside these ranges and needn't reach their ends.
Inputs may be any that keep to these rules, and one draw needn't show every extreme that they name: `utt_lengths`: the first utterance fills all 512 slots and the last has 128 valid frames.
All inputs are finite; a program needn't handle non-finite values.
Results may differ from the reference program's by a relative error of at most 0.0056.
Values may be sent and summed in bfloat16 or wider, within the bound.
A program may use at most 128 MiB of HBM per device.

```python
import math
import jax
import jax.numpy as jnp
from jax import lax

D = 1536
HEADS = 16
KW = 31
K_WO = 23592
K_KERN = 476
BATCH = 8
FRAMES = 512


def draw_queries(key, part):
    base = jnp.clip(jax.random.normal(jax.random.fold_in(key, 11), (BATCH, FRAMES, D), jnp.float32), -6.0, 6.0)
    return base.astype(jnp.bfloat16)


def draw_key_rows(key, part):
    base = jnp.clip(jax.random.normal(jax.random.fold_in(key, 13), (BATCH, FRAMES, D), jnp.float32), -6.0, 6.0)
    return base.astype(jnp.bfloat16)


def draw_utt_lengths(key, part):
    drawn = jax.random.randint(jax.random.fold_in(key, 17), (BATCH,), FRAMES // 4, FRAMES + 1, jnp.int32)
    drawn = drawn.at[0].set(FRAMES)
    drawn = drawn.at[BATCH - 1].set(FRAMES // 4)
    return drawn


def place_ends(values, rng, least, high):
    longest = values.shape.index(max(values.shape))
    spots = []
    for shift in (0, 1):
        where = [jax.random.randint(jax.random.fold_in(rng, axis), (), 0, length) for axis, length in enumerate(values.shape)]
        where[longest] = (where[longest] + shift) % values.shape[longest]
        spots.append(tuple(where))
    return values.at[spots[0]].set(least).at[spots[1]].set(high)


def block_scale(key, dims, shards, least, largest):
    def one(dim, shards_of):
        heights = jax.random.uniform(jax.random.fold_in(jax.random.fold_in(key, 6), dim), (shards_of,), jnp.float32, least / len(shards), largest / len(shards))
        return jnp.repeat(jnp.exp(heights), dims[dim] // shards_of).reshape((-1,) + (1,) * (len(dims) - dim - 1))

    factor_of = one(*shards[0])
    for cut in shards[1:]:
        factor_of = factor_of * one(*cut)
    return factor_of


def normal_values(key, extent, spread, limit, cuts=(), kind=jnp.bfloat16):
    level = block_scale(key, extent, cuts, -0.22, 0.18) if cuts else 1.0
    entries = jax.random.normal(key, extent, jnp.float32) * spread * level
    return jnp.minimum(jnp.maximum(entries, -limit), limit).astype(kind)


def setup_inputs(seed: int = 0) -> dict:
    splits = jax.random.split(jax.random.key(seed), 11)
    return {
        "queries": draw_queries(jax.random.fold_in(splits[10], 71), 0),
        "key_rows": draw_key_rows(jax.random.fold_in(splits[10], 71), 0),
        "value_rows": normal_values(splits[2], (BATCH, FRAMES, D), 1.0, 6.0, ((0, 4), (1, 8))),
        "layer_input": normal_values(splits[3], (BATCH, FRAMES, D), 1.0, 6.0, ((0, 4), (1, 8))),
        "utt_lengths": draw_utt_lengths(jax.random.fold_in(splits[10], 71), 0),
        "out_weight": normal_values(splits[5], (D, D), D ** -0.5, 0.15625),
        "conv_kernel": normal_values(splits[6], (KW, D), KW ** -0.5, 1.0),
        "conv_cotangent": normal_values(splits[7], (BATCH, FRAMES, D), 1.0, 6.0, ((0, 4), (1, 8))),
        "pick_weight": place_ends(jax.random.randint(splits[8], (K_WO,), 0, D * D), jax.random.fold_in(splits[8], 1), 0, (D * D) - 1).astype(jnp.int32),
        "pick_kernel": place_ends(jax.random.randint(splits[9], (K_KERN,), 0, KW * D), jax.random.fold_in(splits[9], 1), 0, (KW * D) - 1).astype(jnp.int32),
    }


neg_big = -1e+30

def reference(queries, key_rows, value_rows, layer_input, utt_lengths, out_weight, conv_kernel, conv_cotangent, pick_weight, pick_kernel):
    head_size = D // HEADS
    score_scale = 1.0 / math.sqrt(head_size)
    frame_ids = jnp.arange(FRAMES, dtype=jnp.int32)
    valid_rows = (frame_ids[None, :] < utt_lengths[:, None]).astype(jnp.float32)

    def split_heads(array):
        return array.reshape(BATCH, FRAMES, HEADS, head_size).transpose(0, 2, 1, 3).reshape(BATCH * HEADS, FRAMES, head_size)
    item_lengths = jnp.repeat(utt_lengths, HEADS)

    def one_item(item):
        query_item, key_item, value_item, length_item = item
        scores = jnp.dot(query_item, key_item.T, preferred_element_type=jnp.float32) * score_scale
        scores = jnp.where((frame_ids < length_item)[None, :], scores, neg_big)
        row_max = lax.optimization_barrier(jnp.max(scores, axis=-1, keepdims=True))
        probs = jnp.exp(scores - row_max)
        weights = probs.astype(jnp.bfloat16)
        denom = lax.optimization_barrier(jnp.sum(probs, axis=-1))
        out_rows = jnp.dot(weights, value_item, preferred_element_type=jnp.float32) / denom[:, None]
        return out_rows.astype(jnp.bfloat16)
    context = lax.map(one_item, (split_heads(queries), split_heads(key_rows), split_heads(value_rows), item_lengths))
    context = context.reshape(BATCH, HEADS, FRAMES, head_size).transpose(0, 2, 1, 3).reshape(BATCH, FRAMES, D)
    context_flat = context.reshape(BATCH * FRAMES, D)
    projected = jnp.dot(context_flat, out_weight, preferred_element_type=jnp.float32).reshape(BATCH, FRAMES, D)
    hidden = ((layer_input.astype(jnp.float32) + projected) * valid_rows[:, :, None]).astype(jnp.bfloat16)
    half_taps = (KW - 1) // 2
    kernel_f = conv_kernel.astype(jnp.float32)
    hidden_pad = jnp.pad(hidden.astype(jnp.float32), ((0, 0), (half_taps, half_taps), (0, 0)))
    cot_f = conv_cotangent.astype(jnp.float32)
    conv_sum = jnp.zeros((BATCH, FRAMES, D), jnp.float32)
    kernel_rows = []
    for offset in range(KW):
        window = hidden_pad[:, offset:offset + FRAMES]
        conv_sum = conv_sum + kernel_f[offset] * window
        kernel_rows.append(lax.optimization_barrier(jnp.sum(window * cot_f, axis=(0, 1))))
    conv_out = conv_sum.astype(jnp.bfloat16)
    kernel_grad = jnp.stack(kernel_rows)
    cot_pad = jnp.pad(cot_f, ((0, 0), (2 * half_taps, 2 * half_taps), (0, 0)))
    back_sum = jnp.zeros((BATCH, FRAMES, D), jnp.float32)
    for offset in range(KW):
        begin = 3 * half_taps - offset
        back_sum = back_sum + kernel_f[offset] * cot_pad[:, begin:begin + FRAMES]
    hidden_grad = (back_sum * valid_rows[:, :, None]).astype(jnp.bfloat16)
    grad_flat = hidden_grad.reshape(BATCH * FRAMES, D)
    weight_grad = lax.dot_general(context_flat, grad_flat, (((0,), (0,)), ((), ())), preferred_element_type=jnp.float32)
    context_grad = lax.dot_general(grad_flat, out_weight, (((1,), (1,)), ((), ())), preferred_element_type=jnp.float32)
    context_grad = context_grad.reshape(BATCH, FRAMES, D).astype(jnp.bfloat16)
    norm_factor = 1.0 / math.sqrt(BATCH * FRAMES)
    weight_picks = weight_grad.reshape(-1)[pick_weight] * norm_factor
    kernel_picks = kernel_grad.reshape(-1)[pick_kernel] * norm_factor
    return (conv_out, context_grad, weight_picks, kernel_picks)
```

```python
import functools
import math

import jax
import jax.numpy as jnp
from jax import lax
from jax.experimental import pallas as pl
from jax.experimental.pallas import tpu as pltpu
from jax.sharding import PartitionSpec as P

HEADS = 16


neg_big = -1e30


def padded(value, sides, width):
    for axis, dim in sides:
        count, length = (lax.axis_size(axis), value.shape[dim])
        up = [(i, (i + 1) % count) for i in range(count - 1)]
        down = [(j, i) for i, j in up]
        last = lax.slice_in_dim(value, length - width, length, axis=dim)
        leading = lax.slice_in_dim(value, 0, width, axis=dim)
        before = lax.ppermute(last, axis, up)
        after = lax.ppermute(leading, axis, down)
        value = jnp.concatenate([before, value, after], axis=dim)
    return value


def softmax_rows(scores, key_ok):
    scores = jnp.where(key_ok, scores, neg_big)
    row_max = jnp.max(scores, axis=-1, keepdims=True)
    probs = jnp.exp(scores - row_max)
    return (probs.astype(jnp.bfloat16), jnp.sum(probs, axis=-1))


def pick_entries(table, picks):
    flat = table.reshape(-1)
    lane = math.gcd(flat.shape[0], 128)
    blocks = flat.reshape(flat.shape[0] // lane, lane)
    chosen = jnp.take(blocks, picks // lane, axis=0)
    lane_ids = jnp.arange(lane, dtype=jnp.int32)
    hit = lane_ids[None, :] == (picks % lane)[:, None]
    return jnp.sum(jnp.where(hit, chosen, jnp.float32(0.0)), axis=1)


def peers_of(axis, count):
    me = lax.axis_index(axis)
    return [lax.rem(me + step, count) for step in range(1, count)]


def greet(axes):
    barrier = pltpu.get_barrier_semaphore()
    total = 0
    for axis, count in axes:
        for peer in peers_of(axis, count):
            pl.semaphore_signal(
                barrier, inc=1, device_id={axis: peer}, device_id_type=pl.DeviceIdType.MESH
            )
            total += 1
    pl.semaphore_wait(barrier, total)


def send_to(src, dst, send_sem, recv_sem, axis, peer):
    copy = pltpu.make_async_remote_copy(
        src_ref=src,
        dst_ref=dst,
        send_sem=send_sem,
        recv_sem=recv_sem,
        device_id={axis: peer},
        device_id_type=pl.DeviceIdType.MESH,
    )
    copy.start()
    return copy


def attention_kernel(
    count,
    score_scale,
    len_ref,
    q_ref,
    k_ref,
    v_ref,
    out_ref,
    send,
    recv,
    back,
    home,
    send_sem,
    recv_sem,
    back_sem,
    home_sem,
):
    utts, frames, width = q_ref.shape
    block = width // count
    head_size = width // HEADS
    me = lax.axis_index("seq")
    greet((("seq", count),))
    for owner in range(count):
        for utt in range(utts):
            for place, ref in enumerate((q_ref, k_ref, v_ref)):
                begin = (utt * 3 + place) * block
                send[owner, :, begin : begin + block] = ref[
                    utt, :, owner * block : (owner + 1) * block
                ]
    copies = [
        send_to(send.at[peer], recv.at[me], send_sem.at[i], recv_sem.at[i], "seq", peer)
        for i, peer in enumerate(peers_of("seq", count))
    ]
    recv[pl.ds(me, 1)] = send[pl.ds(me, 1)]
    for copy in copies:
        copy.wait_recv()
    full = count * frames
    ids = lax.broadcasted_iota(jnp.int32, (full, full), 1)
    for utt in range(utts):
        key_ok = ids < len_ref[utt]
        for head in range(block // head_size):
            parts = []
            for place in range(3):
                begin = (utt * 3 + place) * block + head * head_size
                parts.append(recv[:, :, begin : begin + head_size].reshape(full, head_size))
            query, key, value = parts
            scores = lax.dot_general(
                query, key, (((1,), (1,)), ((), ())), preferred_element_type=jnp.float32
            )
            scores = jnp.where(key_ok, scores * score_scale, neg_big)
            probs = jnp.exp(scores - jnp.max(scores, axis=-1, keepdims=True))
            denom = jnp.sum(probs, axis=-1, keepdims=True)
            rows = jnp.dot(probs.astype(jnp.bfloat16), value, preferred_element_type=jnp.float32)
            rows = (rows / denom).astype(jnp.bfloat16)
            begin = utt * block + head * head_size
            back[:, :, begin : begin + head_size] = rows.reshape(count, frames, head_size)
    returns = [
        send_to(back.at[peer], home.at[me], back_sem.at[i], home_sem.at[i], "seq", peer)
        for i, peer in enumerate(peers_of("seq", count))
    ]
    home[pl.ds(me, 1)] = back[pl.ds(me, 1)]
    for copy in returns:
        copy.wait_recv()
    for owner in range(count):
        for utt in range(utts):
            out_ref[utt, :, owner * block : (owner + 1) * block] = home[
                owner, :, utt * block : (utt + 1) * block
            ]
    for copy in copies + returns:
        copy.wait_send()


def exchanged_attention(queries, key_rows, value_rows, utt_lengths, score_scale):
    utts, frames, width = queries.shape
    count = lax.axis_size("seq")
    block = width // count
    vmem = pl.BlockSpec(memory_space=pltpu.VMEM)
    wide = pltpu.VMEM((count, frames, 3 * utts * block), jnp.bfloat16)
    narrow = pltpu.VMEM((count, frames, utts * block), jnp.bfloat16)
    sems = pltpu.SemaphoreType.DMA((count - 1,))
    return pl.pallas_call(
        functools.partial(attention_kernel, count, score_scale),
        out_shape=jax.ShapeDtypeStruct(queries.shape, jnp.bfloat16),
        in_specs=[pl.BlockSpec(memory_space=pltpu.SMEM), vmem, vmem, vmem],
        out_specs=vmem,
        scratch_shapes=[wide, wide, narrow, narrow, sems, sems, sems, sems],
        compiler_params=pltpu.CompilerParams(
            collective_id=0, has_side_effects=True, vmem_limit_bytes=40 * 2**20
        ),
    )(utt_lengths, queries, key_rows, value_rows)


def total_kernel(
    n_seq, n_dp, x_ref, out_ref, parts, mine, sums, whole, s1, r1, s2, r2, s3, r3
):
    me = lax.axis_index("seq")
    me_dp = lax.axis_index("dp")
    greet((("seq", n_seq), ("dp", n_dp)))
    copies = [
        send_to(x_ref.at[peer], parts.at[me], s1.at[i], r1.at[i], "seq", peer)
        for i, peer in enumerate(peers_of("seq", n_seq))
    ]
    parts[pl.ds(me, 1)] = x_ref[pl.ds(me, 1)]
    for copy in copies:
        copy.wait_recv()
    mine[...] = jnp.sum(parts[...], axis=0)
    second = [
        send_to(mine, sums.at[me_dp], s2.at[i], r2.at[i], "dp", peer)
        for i, peer in enumerate(peers_of("dp", n_dp))
    ]
    sums[pl.ds(me_dp, 1)] = mine[...][None]
    for copy in second:
        copy.wait_recv()
    whole[pl.ds(me, 1)] = jnp.sum(sums[...], axis=0)[None]
    third = [
        send_to(whole.at[me], whole.at[me], s3.at[i], r3.at[i], "seq", peer)
        for i, peer in enumerate(peers_of("seq", n_seq))
    ]
    for copy in third:
        copy.wait_recv()
    out_ref[...] = whole[...]
    for copy in copies + second + third:
        copy.wait_send()


def summed(values):
    n_seq, n_dp = lax.axis_size("seq"), lax.axis_size("dp")
    chunk = 128 * 8 * n_seq
    rows = -(-values.shape[0] // chunk) * 8
    x = jnp.pad(values, (0, rows * 128 * n_seq - values.shape[0])).reshape(n_seq, rows, 128)
    vmem = pl.BlockSpec(memory_space=pltpu.VMEM)
    seq_sems = pltpu.SemaphoreType.DMA((n_seq - 1,))
    dp_sems = pltpu.SemaphoreType.DMA((n_dp - 1,))
    out = pl.pallas_call(
        functools.partial(total_kernel, n_seq, n_dp),
        out_shape=jax.ShapeDtypeStruct(x.shape, jnp.float32),
        in_specs=[vmem],
        out_specs=vmem,
        scratch_shapes=[
            pltpu.VMEM(x.shape, jnp.float32),
            pltpu.VMEM((rows, 128), jnp.float32),
            pltpu.VMEM((n_dp, rows, 128), jnp.float32),
            pltpu.VMEM(x.shape, jnp.float32),
            seq_sems,
            seq_sems,
            dp_sems,
            dp_sems,
            seq_sems,
            seq_sems,
        ],
        compiler_params=pltpu.CompilerParams(collective_id=1, has_side_effects=True),
    )(x)
    return out.reshape(-1)


LOW = 256
PICK_TILE = 512


def choose(stacked, tokens, index):
    low = lax.rem(index, LOW)
    high = lax.div(index, LOW)
    hot = lax.broadcasted_iota(jnp.int32, (LOW, index.shape[1]), 0) == low
    hot = jnp.where(hot, 1.0, 0.0).astype(jnp.bfloat16)
    every = jnp.dot(stacked, hot, preferred_element_type=jnp.float32)
    out = every[:tokens]
    for part in range(1, stacked.shape[0] // tokens):
        out = jnp.where(high == part, every[part * tokens : (part + 1) * tokens], out)
    return out


def picks_kernel(pick_ref, ctx_ref, grad_ref, out_ref, ctx_stack, grad_stack):
    tokens, width = ctx_ref.shape

    @pl.when(pl.program_id(0) == 0)
    def _():
        for part in range(width // LOW):
            cols = slice(part * LOW, (part + 1) * LOW)
            rows = slice(part * tokens, (part + 1) * tokens)
            ctx_stack[rows, :] = ctx_ref[:, cols]
            grad_stack[rows, :] = grad_ref[:, cols]

    pick = pick_ref[...]
    left = choose(ctx_stack[...], tokens, lax.div(pick, width))
    right = choose(grad_stack[...], tokens, lax.rem(pick, width))
    out_ref[...] = jnp.sum(left * right, axis=0, keepdims=True)


def picked_products(ctx, grad, picks):
    tokens, width = ctx.shape
    steps = -(-picks.shape[0] // PICK_TILE)
    padded_picks = jnp.pad(picks, (0, steps * PICK_TILE - picks.shape[0])).reshape(1, -1)
    whole = pl.BlockSpec((tokens, width), lambda i: (0, 0))
    tile = pl.BlockSpec((1, PICK_TILE), lambda i: (0, i))
    stack = pltpu.VMEM((tokens * width // LOW, LOW), jnp.bfloat16)
    out = pl.pallas_call(
        picks_kernel,
        grid=(steps,),
        out_shape=jax.ShapeDtypeStruct(padded_picks.shape, jnp.float32),
        in_specs=[tile, whole, whole],
        out_specs=tile,
        scratch_shapes=[stack, stack],
        compiler_params=pltpu.CompilerParams(vmem_limit_bytes=40 * 2**20),
    )(padded_picks, ctx, grad)
    return out.reshape(-1)


def gathered_attention(queries, key_rows, value_rows, utt_lengths, score_scale):
    local_utts, frames_dev, width = queries.shape
    full_frames = frames_dev * lax.axis_size("seq")
    head_size = width // HEADS
    all_keys, all_values = (
        lax.all_gather(key_rows, "seq", axis=1, tiled=True),
        lax.all_gather(value_rows, "seq", axis=1, tiled=True),
    )
    full_ids = jnp.arange(full_frames, dtype=jnp.int32)

    def one_utt(item):
        query_utt, key_utt, value_utt, length_utt = item
        query_heads = query_utt.reshape(frames_dev, HEADS, head_size)
        key_heads = key_utt.reshape(full_frames, HEADS, head_size)
        value_heads = value_utt.reshape(full_frames, HEADS, head_size)
        scores = (
            jnp.einsum("qhd,khd->hqk", query_heads, key_heads, preferred_element_type=jnp.float32)
            * score_scale
        )
        weights, denom = softmax_rows(scores, (full_ids < length_utt)[None, None, :])
        out_rows = jnp.einsum(
            "hqk,khd->qhd", weights, value_heads, preferred_element_type=jnp.float32
        )
        out_rows = out_rows / denom.transpose(1, 0)[:, :, None]
        return out_rows.astype(jnp.bfloat16).reshape(frames_dev, width)

    return lax.map(one_utt, (queries, all_keys, all_values, utt_lengths))


def on_device(
    queries,
    key_rows,
    value_rows,
    layer_input,
    utt_lengths,
    out_weight,
    conv_kernel,
    conv_cotangent,
    pick_weight,
    pick_kernel,
):
    local_utts, frames_dev, width = queries.shape
    seq_count = lax.axis_size("seq")
    full_frames = frames_dev * seq_count
    head_size = width // HEADS
    score_scale = 1.0 / math.sqrt(head_size)
    first_frame = lax.axis_index("seq") * frames_dev
    local_ids = first_frame + jnp.arange(frames_dev, dtype=jnp.int32)
    valid_rows = (local_ids[None, :] < utt_lengths[:, None]).astype(jnp.float32)
    if HEADS % seq_count == 0:
        context = exchanged_attention(queries, key_rows, value_rows, utt_lengths, score_scale)
    else:
        context = gathered_attention(queries, key_rows, value_rows, utt_lengths, score_scale)
    context_flat = context.reshape(local_utts * frames_dev, width)
    projected = jnp.dot(context_flat, out_weight, preferred_element_type=jnp.float32).reshape(
        local_utts, frames_dev, width
    )
    hidden = ((layer_input.astype(jnp.float32) + projected) * valid_rows[:, :, None]).astype(
        jnp.bfloat16
    )
    tap_count = conv_kernel.shape[0]
    half_taps = (tap_count - 1) // 2
    kernel_f = conv_kernel.astype(jnp.float32)
    hidden_pad = padded(hidden, (("seq", 1),), half_taps)
    cot_f = conv_cotangent.astype(jnp.float32)
    conv_sum = jnp.zeros((local_utts, frames_dev, width), jnp.float32)
    kernel_rows = []
    for offset in range(tap_count):
        window = hidden_pad[:, offset : offset + frames_dev].astype(jnp.float32)
        conv_sum = conv_sum + kernel_f[offset] * window
        kernel_rows.append(jnp.sum(window * cot_f, axis=(0, 1)))
    conv_out = conv_sum.astype(jnp.bfloat16)
    kernel_grad = jnp.stack(kernel_rows)
    cot_pad = padded(conv_cotangent, (("seq", 1),), half_taps).astype(jnp.float32)
    back_sum = jnp.zeros((local_utts, frames_dev, width), jnp.float32)
    for offset in range(tap_count):
        begin = 2 * half_taps - offset
        back_sum = back_sum + kernel_f[offset] * cot_pad[:, begin : begin + frames_dev]
    hidden_grad = (back_sum * valid_rows[:, :, None]).astype(jnp.bfloat16)
    grad_flat = hidden_grad.reshape(local_utts * frames_dev, width)
    context_grad = lax.dot_general(
        grad_flat, out_weight, (((1,), (1,)), ((), ())), preferred_element_type=jnp.float32
    )
    context_grad = context_grad.reshape(local_utts, frames_dev, width).astype(jnp.bfloat16)
    weight_vals = picked_products(context_flat, grad_flat, pick_weight)
    kernel_vals = pick_entries(kernel_grad, pick_kernel)
    total = summed(jnp.concatenate([weight_vals, kernel_vals]))
    weight_sum = total[: pick_weight.shape[0]]
    kernel_sum = total[weight_vals.shape[0] : weight_vals.shape[0] + pick_kernel.shape[0]]
    total_slots = local_utts * lax.axis_size("dp") * full_frames
    norm_factor = 1.0 / math.sqrt(total_slots)
    return (conv_out, context_grad, weight_sum * norm_factor, kernel_sum * norm_factor)


def solution(mesh):
    placed = (
        P("dp", "seq", None),
        P("dp", "seq", None),
        P("dp", "seq", None),
        P("dp", "seq", None),
        P("dp"),
        P(),
        P(),
        P("dp", "seq", None),
        P(),
        P(),
    )
    return jax.shard_map(
        on_device,
        mesh=mesh,
        in_specs=placed,
        out_specs=(P("dp", "seq", None), P("dp", "seq", None), P(), P()),
        check_vma=False,
    )
```

```python
import functools
import math

import jax
import jax.numpy as jnp
from jax import lax
from jax.experimental import pallas as pl
from jax.experimental.pallas import tpu as pltpu
from jax.sharding import PartitionSpec as P

HEADS = 16


neg_big = -1e30


def padded(value, sides, width):
    for axis, dim in sides:
        count, length = (lax.axis_size(axis), value.shape[dim])
        up = [(i, (i + 1) % count) for i in range(count - 1)]
        down = [(j, i) for i, j in up]
        last = lax.slice_in_dim(value, length - width, length, axis=dim)
        leading = lax.slice_in_dim(value, 0, width, axis=dim)
        before = lax.ppermute(last, axis, up)
        after = lax.ppermute(leading, axis, down)
        value = jnp.concatenate([before, value, after], axis=dim)
    return value


def softmax_rows(scores, key_ok):
    scores = jnp.where(key_ok, scores, neg_big)
    row_max = jnp.max(scores, axis=-1, keepdims=True)
    probs = jnp.exp(scores - row_max)
    return (probs.astype(jnp.bfloat16), jnp.sum(probs, axis=-1))


def pick_entries(table, picks):
    flat = table.reshape(-1)
    lane = math.gcd(flat.shape[0], 128)
    blocks = flat.reshape(flat.shape[0] // lane, lane)
    chosen = jnp.take(blocks, picks // lane, axis=0)
    lane_ids = jnp.arange(lane, dtype=jnp.int32)
    hit = lane_ids[None, :] == (picks % lane)[:, None]
    return jnp.sum(jnp.where(hit, chosen, jnp.float32(0.0)), axis=1)


def peers_of(axis, count):
    me = lax.axis_index(axis)
    return [lax.rem(me + step, count) for step in range(1, count)]


def greet(axes):
    barrier = pltpu.get_barrier_semaphore()
    total = 0
    for axis, count in axes:
        for peer in peers_of(axis, count):
            pl.semaphore_signal(
                barrier, inc=1, device_id={axis: peer}, device_id_type=pl.DeviceIdType.MESH
            )
            total += 1
    pl.semaphore_wait(barrier, total)


def send_to(src, dst, send_sem, recv_sem, axis, peer):
    copy = pltpu.make_async_remote_copy(
        src_ref=src,
        dst_ref=dst,
        send_sem=send_sem,
        recv_sem=recv_sem,
        device_id={axis: peer},
        device_id_type=pl.DeviceIdType.MESH,
    )
    copy.start()
    return copy


def total_kernel(
    n_seq, n_dp, x_ref, out_ref, parts, mine, sums, whole, s1, r1, s2, r2, s3, r3
):
    me = lax.axis_index("seq")
    me_dp = lax.axis_index("dp")
    greet((("seq", n_seq), ("dp", n_dp)))
    copies = [
        send_to(x_ref.at[peer], parts.at[me], s1.at[i], r1.at[i], "seq", peer)
        for i, peer in enumerate(peers_of("seq", n_seq))
    ]
    parts[pl.ds(me, 1)] = x_ref[pl.ds(me, 1)]
    for copy in copies:
        copy.wait_recv()
    mine[...] = jnp.sum(parts[...], axis=0)
    second = [
        send_to(mine, sums.at[me_dp], s2.at[i], r2.at[i], "dp", peer)
        for i, peer in enumerate(peers_of("dp", n_dp))
    ]
    sums[pl.ds(me_dp, 1)] = mine[...][None]
    for copy in second:
        copy.wait_recv()
    whole[pl.ds(me, 1)] = jnp.sum(sums[...], axis=0)[None]
    third = [
        send_to(whole.at[me], whole.at[me], s3.at[i], r3.at[i], "seq", peer)
        for i, peer in enumerate(peers_of("seq", n_seq))
    ]
    for copy in third:
        copy.wait_recv()
    out_ref[...] = whole[...]
    for copy in copies + second + third:
        copy.wait_send()


def summed(values):
    n_seq, n_dp = lax.axis_size("seq"), lax.axis_size("dp")
    chunk = 128 * 8 * n_seq
    rows = -(-values.shape[0] // chunk) * 8
    x = jnp.pad(values, (0, rows * 128 * n_seq - values.shape[0])).reshape(n_seq, rows, 128)
    vmem = pl.BlockSpec(memory_space=pltpu.VMEM)
    seq_sems = pltpu.SemaphoreType.DMA((n_seq - 1,))
    dp_sems = pltpu.SemaphoreType.DMA((n_dp - 1,))
    out = pl.pallas_call(
        functools.partial(total_kernel, n_seq, n_dp),
        out_shape=jax.ShapeDtypeStruct(x.shape, jnp.float32),
        in_specs=[vmem],
        out_specs=vmem,
        scratch_shapes=[
            pltpu.VMEM(x.shape, jnp.float32),
            pltpu.VMEM((rows, 128), jnp.float32),
            pltpu.VMEM((n_dp, rows, 128), jnp.float32),
            pltpu.VMEM(x.shape, jnp.float32),
            seq_sems,
            seq_sems,
            dp_sems,
            dp_sems,
            seq_sems,
            seq_sems,
        ],
        compiler_params=pltpu.CompilerParams(collective_id=1, has_side_effects=True),
    )(x)
    return out.reshape(-1)


LOW = 256
PICK_TILE = 512


def choose(stacked, tokens, index):
    low = lax.rem(index, LOW)
    high = lax.div(index, LOW)
    hot = lax.broadcasted_iota(jnp.int32, (LOW, index.shape[1]), 0) == low
    hot = jnp.where(hot, 1.0, 0.0).astype(jnp.bfloat16)
    every = jnp.dot(stacked, hot, preferred_element_type=jnp.float32)
    out = every[:tokens]
    for part in range(1, stacked.shape[0] // tokens):
        out = jnp.where(high == part, every[part * tokens : (part + 1) * tokens], out)
    return out


def picks_kernel(pick_ref, ctx_ref, grad_ref, out_ref, ctx_stack, grad_stack):
    tokens, width = ctx_ref.shape

    @pl.when(pl.program_id(0) == 0)
    def _():
        for part in range(width // LOW):
            cols = slice(part * LOW, (part + 1) * LOW)
            rows = slice(part * tokens, (part + 1) * tokens)
            ctx_stack[rows, :] = ctx_ref[:, cols]
            grad_stack[rows, :] = grad_ref[:, cols]

    pick = pick_ref[...]
    left = choose(ctx_stack[...], tokens, lax.div(pick, width))
    right = choose(grad_stack[...], tokens, lax.rem(pick, width))
    out_ref[...] = jnp.sum(left * right, axis=0, keepdims=True)


def picked_products(ctx, grad, picks):
    tokens, width = ctx.shape
    steps = -(-picks.shape[0] // PICK_TILE)
    padded_picks = jnp.pad(picks, (0, steps * PICK_TILE - picks.shape[0])).reshape(1, -1)
    whole = pl.BlockSpec((tokens, width), lambda i: (0, 0))
    tile = pl.BlockSpec((1, PICK_TILE), lambda i: (0, i))
    stack = pltpu.VMEM((tokens * width // LOW, LOW), jnp.bfloat16)
    out = pl.pallas_call(
        picks_kernel,
        grid=(steps,),
        out_shape=jax.ShapeDtypeStruct(padded_picks.shape, jnp.float32),
        in_specs=[tile, whole, whole],
        out_specs=tile,
        scratch_shapes=[stack, stack],
        compiler_params=pltpu.CompilerParams(vmem_limit_bytes=40 * 2**20),
    )(padded_picks, ctx, grad)
    return out.reshape(-1)


def gathered_attention(queries, key_rows, value_rows, utt_lengths, score_scale):
    local_utts, frames_dev, width = queries.shape
    full_frames = frames_dev * lax.axis_size("seq")
    head_size = width // HEADS
    all_keys, all_values = (
        lax.all_gather(key_rows, "seq", axis=1, tiled=True),
        lax.all_gather(value_rows, "seq", axis=1, tiled=True),
    )
    full_ids = jnp.arange(full_frames, dtype=jnp.int32)

    def one_utt(item):
        query_utt, key_utt, value_utt, length_utt = item
        query_heads = query_utt.reshape(frames_dev, HEADS, head_size)
        key_heads = key_utt.reshape(full_frames, HEADS, head_size)
        value_heads = value_utt.reshape(full_frames, HEADS, head_size)
        scores = (
            jnp.einsum("qhd,khd->hqk", query_heads, key_heads, preferred_element_type=jnp.float32)
            * score_scale
        )
        weights, denom = softmax_rows(scores, (full_ids < length_utt)[None, None, :])
        out_rows = jnp.einsum(
            "hqk,khd->qhd", weights, value_heads, preferred_element_type=jnp.float32
        )
        out_rows = out_rows / denom.transpose(1, 0)[:, :, None]
        return out_rows.astype(jnp.bfloat16).reshape(frames_dev, width)

    return lax.map(one_utt, (queries, all_keys, all_values, utt_lengths))


def shifted_windows(chunk, frames):
    for turn in range(8):
        part = chunk[turn : turn + frames + 24]
        for eight in range(4):
            offset = 8 * eight + turn
            if 1 <= offset <= 31:
                yield offset, part[8 * eight : 8 * eight + frames]


def block_kernel(
    n_seq,
    n_dp,
    rows_each,
    score_scale,
    norm_factor,
    len_ref,
    pick_ref,
    kern_ref,
    q_hbm,
    k_hbm,
    v_hbm,
    in_hbm,
    cot_hbm,
    w_hbm,
    conv_ref,
    cgrad_ref,
    sum_ref,
    q_ref,
    k_ref,
    v_ref,
    in_ref,
    cot_ref,
    w_ref,
    send,
    recv,
    back,
    home,
    cot_edge,
    hid_edge,
    cot_pad,
    hid_pad,
    hidden,
    grad,
    grad_stack,
    ctx,
    ctx_stack,
    grad_picked,
    kern_grad,
    x_ref,
    parts,
    mine,
    sums,
    whole,
    load_sem,
    send_sem,
    recv_sem,
    back_sem,
    home_sem,
    edge_send,
    edge_recv,
    s1,
    r1,
    s2,
    r2,
    s3,
    r3,
):
    utts, frames, width = q_ref.shape
    taps = kern_ref.shape[0]
    reach = 16
    tokens = utts * frames
    block = width // n_seq
    head_size = width // HEADS
    me = lax.axis_index("seq")
    me_dp = lax.axis_index("dp")
    right, left = lax.rem(me + 1, n_seq), lax.rem(me + n_seq - 1, n_seq)
    loads = [
        pltpu.make_async_copy(src, dst, load_sem.at[i])
        for i, (src, dst) in enumerate(
            (
                (cot_hbm, cot_ref),
                (q_hbm, q_ref),
                (k_hbm, k_ref),
                (v_hbm, v_ref),
                (w_hbm, w_ref),
                (in_hbm, in_ref),
            )
        )
    ]
    for load in loads:
        load.start()
    greet((("seq", n_seq), ("dp", n_dp)))

    def swap_edges(rows, edge, base):
        return [
            send_to(
                rows.at[:, frames - reach : frames],
                edge.at[0],
                edge_send.at[base],
                edge_recv.at[base],
                "seq",
                right,
            ),
            send_to(
                rows.at[:, 0:reach],
                edge.at[1],
                edge_send.at[base + 1],
                edge_recv.at[base + 1],
                "seq",
                left,
            ),
        ]

    def pad_edges(edge, pad):
        for utt in range(utts):
            before = edge[0, utt].astype(jnp.float32)
            after = edge[1, utt].astype(jnp.float32)
            pad[utt, 0:reach, :] = jnp.where(me > 0, before, 0.0)
            pad[utt, reach + frames : 2 * reach + frames, :] = jnp.where(
                me < n_seq - 1, after, 0.0
            )

    for load in loads[:4]:
        load.wait()
    for owner in range(n_seq):
        for utt in range(utts):
            for place, ref in enumerate((q_ref, k_ref, v_ref)):
                begin = (utt * 3 + place) * block
                send[owner, :, begin : begin + block] = ref[
                    utt, :, owner * block : (owner + 1) * block
                ]
    edges = swap_edges(cot_ref, cot_edge, 0)
    copies = [
        send_to(send.at[peer], recv.at[me], send_sem.at[i], recv_sem.at[i], "seq", peer)
        for i, peer in enumerate(peers_of("seq", n_seq))
    ]
    recv[pl.ds(me, 1)] = send[pl.ds(me, 1)]

    frame_ids = me * frames + lax.broadcasted_iota(jnp.int32, (frames, 1), 0)
    for utt in range(utts):
        cot_pad[utt, reach : reach + frames, :] = cot_ref[utt].astype(jnp.float32)
    for copy in edges:
        copy.wait_recv()
    pad_edges(cot_edge, cot_pad)

    @pl.loop(0, width // 128)
    def _(step):
        cols = pl.ds(pl.multiple_of(step * 128, 128), 128)
        kern = kern_ref[:, cols].astype(jnp.float32)
        for utt in range(utts):
            total = jnp.zeros((frames, 128), jnp.float32)
            for offset, window in shifted_windows(cot_pad[utt, :, cols], frames):
                tap = taps - offset
                total = total + kern[tap : tap + 1] * window
            total = jnp.where(frame_ids < len_ref[utt], total, 0.0)
            grad[utt * frames : (utt + 1) * frames, cols] = total.astype(jnp.bfloat16)

    for part in range(width // LOW):
        grad_stack[part * tokens : (part + 1) * tokens, :] = grad[
            :, part * LOW : (part + 1) * LOW
        ]

    @pl.loop(0, n_seq)
    def _(owner):
        for row in range(rows_each):
            pick = pick_ref[owner, row : row + 1, :]
            found = choose(grad_stack[...], tokens, lax.rem(pick, width))
            grad_picked[owner, row] = found.astype(jnp.bfloat16)

    loads[4].wait()
    loads[5].wait()

    @pl.loop(0, width // LOW)
    def _(step):
        cols = pl.ds(pl.multiple_of(step * LOW, LOW), LOW)
        value = lax.dot_general(
            grad[...], w_ref[cols, :], (((1,), (1,)), ((), ())), preferred_element_type=jnp.float32
        ).astype(jnp.bfloat16)
        for utt in range(utts):
            cgrad_ref[utt, :, cols] = value[utt * frames : (utt + 1) * frames]

    for copy in copies:
        copy.wait_recv()
    full = n_seq * frames
    ids = lax.broadcasted_iota(jnp.int32, (full, full), 1)
    for utt in range(utts):
        key_ok = ids < len_ref[utt]
        for head in range(block // head_size):
            three = []
            for place in range(3):
                begin = (utt * 3 + place) * block + head * head_size
                three.append(recv[:, :, begin : begin + head_size].reshape(full, head_size))
            query, key, value = three
            scores = lax.dot_general(
                query, key, (((1,), (1,)), ((), ())), preferred_element_type=jnp.float32
            )
            scores = jnp.where(key_ok, scores * score_scale, neg_big)
            probs = jnp.exp(scores - jnp.max(scores, axis=-1, keepdims=True))
            denom = jnp.sum(probs, axis=-1, keepdims=True)
            rows = jnp.dot(probs.astype(jnp.bfloat16), value, preferred_element_type=jnp.float32)
            rows = (rows / denom).astype(jnp.bfloat16)
            begin = utt * block + head * head_size
            back[:, :, begin : begin + head_size] = rows.reshape(n_seq, frames, head_size)
    returns = [
        send_to(back.at[peer], home.at[me], back_sem.at[i], home_sem.at[i], "seq", peer)
        for i, peer in enumerate(peers_of("seq", n_seq))
    ]
    home[pl.ds(me, 1)] = back[pl.ds(me, 1)]
    for copy in returns:
        copy.wait_recv()
    for owner in range(n_seq):
        for utt in range(utts):
            ctx[utt * frames : (utt + 1) * frames, owner * block : (owner + 1) * block] = home[
                owner, :, utt * block : (utt + 1) * block
            ]

    @pl.loop(0, width // LOW)
    def _(step):
        cols = pl.ds(pl.multiple_of(step * LOW, LOW), LOW)
        value = jnp.dot(ctx[...], w_ref[:, cols], preferred_element_type=jnp.float32)
        for utt in range(utts):
            rows = in_ref[utt, :, cols].astype(jnp.float32)
            rows = rows + value[utt * frames : (utt + 1) * frames]
            rows = jnp.where(frame_ids < len_ref[utt], rows, 0.0).astype(jnp.bfloat16)
            hidden[utt, :, cols] = rows
            hid_pad[utt, reach : reach + frames, cols] = rows.astype(jnp.float32)

    hid_copies = swap_edges(hidden, hid_edge, 2)
    for part in range(width // LOW):
        ctx_stack[part * tokens : (part + 1) * tokens, :] = ctx[:, part * LOW : (part + 1) * LOW]

    @pl.loop(0, n_seq)
    def _(owner):
        for row in range(rows_each):
            pick = pick_ref[owner, row : row + 1, :]
            found = choose(ctx_stack[...], tokens, lax.div(pick, width))
            found = found * grad_picked[owner, row].astype(jnp.float32)
            x_ref[owner, row : row + 1, :] = jnp.sum(found, axis=0, keepdims=True)

    for copy in hid_copies:
        copy.wait_recv()
    pad_edges(hid_edge, hid_pad)
    kern_grad[...] = jnp.zeros_like(kern_grad)

    @pl.loop(0, width // 128)
    def _(step):
        cols = pl.ds(pl.multiple_of(step * 128, 128), 128)
        found = {}
        for utt in range(utts):
            cot = cot_pad[utt, reach : reach + frames, cols]
            for offset, window in shifted_windows(hid_pad[utt, :, cols], frames):
                value = jnp.sum((window * cot).reshape(frames // 8, 8, 128), axis=0)
                found[offset] = value if utt == 0 else found[offset] + value
        for offset, value in found.items():
            kern_grad[offset - 1 : offset, cols] = jnp.sum(value, axis=0, keepdims=True)

    pick = pick_ref[n_seq - 1, rows_each - 1 : rows_each, :]
    rest = jnp.concatenate(
        [kern_grad[:, part * LOW : (part + 1) * LOW] for part in range(width // LOW)], axis=0
    )
    found = jnp.zeros((kern_grad.shape[0], PICK_TILE), jnp.float32)
    for _ in range(3):
        piece = rest.astype(jnp.bfloat16)
        rest = rest - piece.astype(jnp.float32)
        found = found + choose(piece, kern_grad.shape[0], lax.rem(pick, width))
    tap_ids = lax.broadcasted_iota(jnp.int32, found.shape, 0)
    found = jnp.where(tap_ids == lax.div(pick, width), found, 0.0)
    x_ref[n_seq - 1, rows_each - 1 : rows_each, :] = jnp.sum(found, axis=0, keepdims=True)

    first = [
        send_to(x_ref.at[peer], parts.at[me], s1.at[i], r1.at[i], "seq", peer)
        for i, peer in enumerate(peers_of("seq", n_seq))
    ]
    parts[pl.ds(me, 1)] = x_ref[pl.ds(me, 1)]

    @pl.loop(0, width // 128)
    def _(step):
        cols = pl.ds(pl.multiple_of(step * 128, 128), 128)
        kern = kern_ref[:, cols].astype(jnp.float32)
        for utt in range(utts):
            total = jnp.zeros((frames, 128), jnp.float32)
            for offset, window in shifted_windows(hid_pad[utt, :, cols], frames):
                total = total + kern[offset - 1 : offset] * window
            conv_ref[utt, :, cols] = total.astype(jnp.bfloat16)

    for copy in first:
        copy.wait_recv()
    mine[...] = jnp.sum(parts[...], axis=0)
    second = [
        send_to(mine, sums.at[me_dp], s2.at[i], r2.at[i], "dp", peer)
        for i, peer in enumerate(peers_of("dp", n_dp))
    ]
    sums[pl.ds(me_dp, 1)] = mine[...][None]
    for copy in second:
        copy.wait_recv()
    whole[pl.ds(me, 1)] = (jnp.sum(sums[...], axis=0) * norm_factor)[None]
    third = [
        send_to(whole.at[me], whole.at[me], s3.at[i], r3.at[i], "seq", peer)
        for i, peer in enumerate(peers_of("seq", n_seq))
    ]
    for copy in third:
        copy.wait_recv()
    for owner in range(n_seq):
        sum_ref[owner * rows_each : (owner + 1) * rows_each] = whole[owner, 0:rows_each]
    for copy in edges + copies + returns + hid_copies + first + second + third:
        copy.wait_send()


def one_kernel(
    queries,
    key_rows,
    value_rows,
    layer_input,
    utt_lengths,
    out_weight,
    conv_kernel,
    conv_cotangent,
    pick_weight,
    pick_kernel,
):
    utts, frames, width = queries.shape
    n_seq, n_dp = lax.axis_size("seq"), lax.axis_size("dp")
    block = width // n_seq
    tokens = utts * frames
    tiles = -(-pick_weight.shape[0] // PICK_TILE) + 1
    rows_each = -(-tiles // n_seq)
    kernel_start = (rows_each * n_seq - 1) * PICK_TILE
    picks = jnp.concatenate(
        [
            jnp.pad(pick_weight, (0, kernel_start - pick_weight.shape[0])),
            jnp.pad(pick_kernel, (0, PICK_TILE - pick_kernel.shape[0])),
        ]
    ).reshape(n_seq, rows_each, PICK_TILE)
    held_rows = -(-rows_each // 8) * 8
    vmem = pl.BlockSpec(memory_space=pltpu.VMEM)
    hbm = pl.BlockSpec(memory_space=pl.ANY)
    bf16, f32 = jnp.bfloat16, jnp.float32
    local = pltpu.VMEM((utts, frames, width), bf16)
    wide = pltpu.VMEM((n_seq, frames, 3 * utts * block), bf16)
    narrow = pltpu.VMEM((n_seq, frames, utts * block), bf16)
    edge = pltpu.VMEM((2, utts, 16, width), bf16)
    pad = pltpu.VMEM((utts, frames + 32, width), f32)
    flat = pltpu.VMEM((tokens, width), bf16)
    stack = pltpu.VMEM((tokens * width // LOW, LOW), bf16)
    partial = pltpu.VMEM((n_seq, held_rows, PICK_TILE), f32)
    seq_sems = pltpu.SemaphoreType.DMA((n_seq - 1,))
    dp_sems = pltpu.SemaphoreType.DMA((n_dp - 1,))
    score_scale = 1.0 / math.sqrt(width // HEADS)
    norm_factor = 1.0 / math.sqrt(utts * n_dp * frames * n_seq)
    conv_out, context_grad, total = pl.pallas_call(
        functools.partial(block_kernel, n_seq, n_dp, rows_each, score_scale, norm_factor),
        out_shape=(
            jax.ShapeDtypeStruct(queries.shape, bf16),
            jax.ShapeDtypeStruct(queries.shape, bf16),
            jax.ShapeDtypeStruct((n_seq * rows_each, PICK_TILE), f32),
        ),
        in_specs=[pl.BlockSpec(memory_space=pltpu.SMEM), vmem, vmem] + [hbm] * 6,
        out_specs=(vmem, vmem, vmem),
        scratch_shapes=[
            local,
            local,
            local,
            local,
            local,
            pltpu.VMEM((width, width), bf16),
            wide,
            wide,
            narrow,
            narrow,
            edge,
            edge,
            pad,
            pad,
            local,
            flat,
            stack,
            flat,
            stack,
            pltpu.VMEM((n_seq, rows_each, tokens, PICK_TILE), bf16),
            pltpu.VMEM((32, width), f32),
            partial,
            partial,
            pltpu.VMEM((held_rows, PICK_TILE), f32),
            pltpu.VMEM((n_dp, held_rows, PICK_TILE), f32),
            partial,
            pltpu.SemaphoreType.DMA((6,)),
            seq_sems,
            seq_sems,
            seq_sems,
            seq_sems,
            pltpu.SemaphoreType.DMA((4,)),
            pltpu.SemaphoreType.DMA((4,)),
            seq_sems,
            seq_sems,
            dp_sems,
            dp_sems,
            seq_sems,
            seq_sems,
        ],
        compiler_params=pltpu.CompilerParams(
            collective_id=2, has_side_effects=True, vmem_limit_bytes=56 * 2**20
        ),
    )(
        utt_lengths,
        picks,
        conv_kernel,
        queries,
        key_rows,
        value_rows,
        layer_input,
        conv_cotangent,
        out_weight,
    )
    flat_total = total.reshape(-1)
    weight_picks = flat_total[: pick_weight.shape[0]]
    kernel_picks = flat_total[kernel_start : kernel_start + pick_kernel.shape[0]]
    return (conv_out, context_grad, weight_picks, kernel_picks)


def on_device(
    queries,
    key_rows,
    value_rows,
    layer_input,
    utt_lengths,
    out_weight,
    conv_kernel,
    conv_cotangent,
    pick_weight,
    pick_kernel,
):
    local_utts, frames_dev, width = queries.shape
    seq_count = lax.axis_size("seq")
    if HEADS % seq_count == 0:
        return one_kernel(
            queries,
            key_rows,
            value_rows,
            layer_input,
            utt_lengths,
            out_weight,
            conv_kernel,
            conv_cotangent,
            pick_weight,
            pick_kernel,
        )
    full_frames = frames_dev * seq_count
    head_size = width // HEADS
    score_scale = 1.0 / math.sqrt(head_size)
    first_frame = lax.axis_index("seq") * frames_dev
    local_ids = first_frame + jnp.arange(frames_dev, dtype=jnp.int32)
    valid_rows = (local_ids[None, :] < utt_lengths[:, None]).astype(jnp.float32)
    context = gathered_attention(queries, key_rows, value_rows, utt_lengths, score_scale)
    context_flat = context.reshape(local_utts * frames_dev, width)
    projected = jnp.dot(context_flat, out_weight, preferred_element_type=jnp.float32).reshape(
        local_utts, frames_dev, width
    )
    hidden = ((layer_input.astype(jnp.float32) + projected) * valid_rows[:, :, None]).astype(
        jnp.bfloat16
    )
    tap_count = conv_kernel.shape[0]
    half_taps = (tap_count - 1) // 2
    kernel_f = conv_kernel.astype(jnp.float32)
    hidden_pad = padded(hidden, (("seq", 1),), half_taps)
    cot_f = conv_cotangent.astype(jnp.float32)
    conv_sum = jnp.zeros((local_utts, frames_dev, width), jnp.float32)
    kernel_rows = []
    for offset in range(tap_count):
        window = hidden_pad[:, offset : offset + frames_dev].astype(jnp.float32)
        conv_sum = conv_sum + kernel_f[offset] * window
        kernel_rows.append(jnp.sum(window * cot_f, axis=(0, 1)))
    conv_out = conv_sum.astype(jnp.bfloat16)
    kernel_grad = jnp.stack(kernel_rows)
    cot_pad = padded(conv_cotangent, (("seq", 1),), half_taps).astype(jnp.float32)
    back_sum = jnp.zeros((local_utts, frames_dev, width), jnp.float32)
    for offset in range(tap_count):
        begin = 2 * half_taps - offset
        back_sum = back_sum + kernel_f[offset] * cot_pad[:, begin : begin + frames_dev]
    hidden_grad = (back_sum * valid_rows[:, :, None]).astype(jnp.bfloat16)
    grad_flat = hidden_grad.reshape(local_utts * frames_dev, width)
    context_grad = lax.dot_general(
        grad_flat, out_weight, (((1,), (1,)), ((), ())), preferred_element_type=jnp.float32
    )
    context_grad = context_grad.reshape(local_utts, frames_dev, width).astype(jnp.bfloat16)
    weight_vals = picked_products(context_flat, grad_flat, pick_weight)
    kernel_vals = pick_entries(kernel_grad, pick_kernel)
    total = summed(jnp.concatenate([weight_vals, kernel_vals]))
    weight_sum = total[: pick_weight.shape[0]]
    kernel_sum = total[weight_vals.shape[0] : weight_vals.shape[0] + pick_kernel.shape[0]]
    total_slots = local_utts * lax.axis_size("dp") * full_frames
    norm_factor = 1.0 / math.sqrt(total_slots)
    return (conv_out, context_grad, weight_sum * norm_factor, kernel_sum * norm_factor)


def solution(mesh):
    placed = (
        P("dp", "seq", None),
        P("dp", "seq", None),
        P("dp", "seq", None),
        P("dp", "seq", None),
        P("dp"),
        P(),
        P(),
        P("dp", "seq", None),
        P(),
        P(),
    )
    return jax.shard_map(
        on_device,
        mesh=mesh,
        in_specs=placed,
        out_specs=(P("dp", "seq", None), P("dp", "seq", None), P(), P()),
        check_vma=False,
    )
```

```python
import functools
import math

import jax
import jax.numpy as jnp
from jax import lax
from jax.experimental import pallas as pl
from jax.experimental.pallas import tpu as pltpu
from jax.sharding import PartitionSpec as P

HEADS = 16


neg_big = -1e30


def padded(value, sides, width):
    for axis, dim in sides:
        count, length = (lax.axis_size(axis), value.shape[dim])
        up = [(i, (i + 1) % count) for i in range(count - 1)]
        down = [(j, i) for i, j in up]
        last = lax.slice_in_dim(value, length - width, length, axis=dim)
        leading = lax.slice_in_dim(value, 0, width, axis=dim)
        before = lax.ppermute(last, axis, up)
        after = lax.ppermute(leading, axis, down)
        value = jnp.concatenate([before, value, after], axis=dim)
    return value


def softmax_rows(scores, key_ok):
    scores = jnp.where(key_ok, scores, neg_big)
    row_max = jnp.max(scores, axis=-1, keepdims=True)
    probs = jnp.exp(scores - row_max)
    return (probs.astype(jnp.bfloat16), jnp.sum(probs, axis=-1))


def pick_entries(table, picks):
    flat = table.reshape(-1)
    lane = math.gcd(flat.shape[0], 128)
    blocks = flat.reshape(flat.shape[0] // lane, lane)
    chosen = jnp.take(blocks, picks // lane, axis=0)
    lane_ids = jnp.arange(lane, dtype=jnp.int32)
    hit = lane_ids[None, :] == (picks % lane)[:, None]
    return jnp.sum(jnp.where(hit, chosen, jnp.float32(0.0)), axis=1)


def peers_of(axis, count):
    me = lax.axis_index(axis)
    return [lax.rem(me + step, count) for step in range(1, count)]


def greet(axes):
    barrier = pltpu.get_barrier_semaphore()
    total = 0
    for axis, count in axes:
        for peer in peers_of(axis, count):
            pl.semaphore_signal(
                barrier, inc=1, device_id={axis: peer}, device_id_type=pl.DeviceIdType.MESH
            )
            total += 1
    pl.semaphore_wait(barrier, total)


def send_to(src, dst, send_sem, recv_sem, axis, peer):
    copy = pltpu.make_async_remote_copy(
        src_ref=src,
        dst_ref=dst,
        send_sem=send_sem,
        recv_sem=recv_sem,
        device_id={axis: peer},
        device_id_type=pl.DeviceIdType.MESH,
    )
    copy.start()
    return copy


def total_kernel(
    n_seq, n_dp, x_ref, out_ref, parts, mine, sums, whole, s1, r1, s2, r2, s3, r3
):
    me = lax.axis_index("seq")
    me_dp = lax.axis_index("dp")
    greet((("seq", n_seq), ("dp", n_dp)))
    copies = [
        send_to(x_ref.at[peer], parts.at[me], s1.at[i], r1.at[i], "seq", peer)
        for i, peer in enumerate(peers_of("seq", n_seq))
    ]
    parts[pl.ds(me, 1)] = x_ref[pl.ds(me, 1)]
    for copy in copies:
        copy.wait_recv()
    mine[...] = jnp.sum(parts[...], axis=0)
    second = [
        send_to(mine, sums.at[me_dp], s2.at[i], r2.at[i], "dp", peer)
        for i, peer in enumerate(peers_of("dp", n_dp))
    ]
    sums[pl.ds(me_dp, 1)] = mine[...][None]
    for copy in second:
        copy.wait_recv()
    whole[pl.ds(me, 1)] = jnp.sum(sums[...], axis=0)[None]
    third = [
        send_to(whole.at[me], whole.at[me], s3.at[i], r3.at[i], "seq", peer)
        for i, peer in enumerate(peers_of("seq", n_seq))
    ]
    for copy in third:
        copy.wait_recv()
    out_ref[...] = whole[...]
    for copy in copies + second + third:
        copy.wait_send()


def summed(values):
    n_seq, n_dp = lax.axis_size("seq"), lax.axis_size("dp")
    chunk = 128 * 8 * n_seq
    rows = -(-values.shape[0] // chunk) * 8
    x = jnp.pad(values, (0, rows * 128 * n_seq - values.shape[0])).reshape(n_seq, rows, 128)
    vmem = pl.BlockSpec(memory_space=pltpu.VMEM)
    seq_sems = pltpu.SemaphoreType.DMA((n_seq - 1,))
    dp_sems = pltpu.SemaphoreType.DMA((n_dp - 1,))
    out = pl.pallas_call(
        functools.partial(total_kernel, n_seq, n_dp),
        out_shape=jax.ShapeDtypeStruct(x.shape, jnp.float32),
        in_specs=[vmem],
        out_specs=vmem,
        scratch_shapes=[
            pltpu.VMEM(x.shape, jnp.float32),
            pltpu.VMEM((rows, 128), jnp.float32),
            pltpu.VMEM((n_dp, rows, 128), jnp.float32),
            pltpu.VMEM(x.shape, jnp.float32),
            seq_sems,
            seq_sems,
            dp_sems,
            dp_sems,
            seq_sems,
            seq_sems,
        ],
        compiler_params=pltpu.CompilerParams(collective_id=1, has_side_effects=True),
    )(x)
    return out.reshape(-1)


LOW = 256
PICK_TILE = 512


def choose(stacked, tokens, index):
    low = lax.rem(index, LOW)
    high = lax.div(index, LOW)
    hot = lax.broadcasted_iota(jnp.int32, (LOW, index.shape[1]), 0) == low
    hot = jnp.where(hot, 1.0, 0.0).astype(jnp.bfloat16)
    every = jnp.dot(stacked, hot, preferred_element_type=jnp.float32)
    out = every[:tokens]
    for part in range(1, stacked.shape[0] // tokens):
        out = jnp.where(high == part, every[part * tokens : (part + 1) * tokens], out)
    return out


def picks_kernel(pick_ref, ctx_ref, grad_ref, out_ref, ctx_stack, grad_stack):
    tokens, width = ctx_ref.shape

    @pl.when(pl.program_id(0) == 0)
    def _():
        for part in range(width // LOW):
            cols = slice(part * LOW, (part + 1) * LOW)
            rows = slice(part * tokens, (part + 1) * tokens)
            ctx_stack[rows, :] = ctx_ref[:, cols]
            grad_stack[rows, :] = grad_ref[:, cols]

    pick = pick_ref[...]
    left = choose(ctx_stack[...], tokens, lax.div(pick, width))
    right = choose(grad_stack[...], tokens, lax.rem(pick, width))
    out_ref[...] = jnp.sum(left * right, axis=0, keepdims=True)


def picked_products(ctx, grad, picks):
    tokens, width = ctx.shape
    steps = -(-picks.shape[0] // PICK_TILE)
    padded_picks = jnp.pad(picks, (0, steps * PICK_TILE - picks.shape[0])).reshape(1, -1)
    whole = pl.BlockSpec((tokens, width), lambda i: (0, 0))
    tile = pl.BlockSpec((1, PICK_TILE), lambda i: (0, i))
    stack = pltpu.VMEM((tokens * width // LOW, LOW), jnp.bfloat16)
    out = pl.pallas_call(
        picks_kernel,
        grid=(steps,),
        out_shape=jax.ShapeDtypeStruct(padded_picks.shape, jnp.float32),
        in_specs=[tile, whole, whole],
        out_specs=tile,
        scratch_shapes=[stack, stack],
        compiler_params=pltpu.CompilerParams(vmem_limit_bytes=40 * 2**20),
    )(padded_picks, ctx, grad)
    return out.reshape(-1)


def gathered_attention(queries, key_rows, value_rows, utt_lengths, score_scale):
    local_utts, frames_dev, width = queries.shape
    full_frames = frames_dev * lax.axis_size("seq")
    head_size = width // HEADS
    all_keys, all_values = (
        lax.all_gather(key_rows, "seq", axis=1, tiled=True),
        lax.all_gather(value_rows, "seq", axis=1, tiled=True),
    )
    full_ids = jnp.arange(full_frames, dtype=jnp.int32)

    def one_utt(item):
        query_utt, key_utt, value_utt, length_utt = item
        query_heads = query_utt.reshape(frames_dev, HEADS, head_size)
        key_heads = key_utt.reshape(full_frames, HEADS, head_size)
        value_heads = value_utt.reshape(full_frames, HEADS, head_size)
        scores = (
            jnp.einsum("qhd,khd->hqk", query_heads, key_heads, preferred_element_type=jnp.float32)
            * score_scale
        )
        weights, denom = softmax_rows(scores, (full_ids < length_utt)[None, None, :])
        out_rows = jnp.einsum(
            "hqk,khd->qhd", weights, value_heads, preferred_element_type=jnp.float32
        )
        out_rows = out_rows / denom.transpose(1, 0)[:, :, None]
        return out_rows.astype(jnp.bfloat16).reshape(frames_dev, width)

    return lax.map(one_utt, (queries, all_keys, all_values, utt_lengths))


def shifted_windows(chunk, frames):
    for turn in range(8):
        part = chunk[turn : turn + frames + 24]
        for eight in range(4):
            offset = 8 * eight + turn
            if 1 <= offset <= 31:
                yield offset, part[8 * eight : 8 * eight + frames]


def block_kernel(
    n_seq,
    n_dp,
    rows_each,
    score_scale,
    norm_factor,
    len_ref,
    pick_ref,
    kern_ref,
    q_hbm,
    k_hbm,
    v_hbm,
    in_hbm,
    cot_hbm,
    w_hbm,
    conv_ref,
    cgrad_ref,
    sum_ref,
    q_ref,
    k_ref,
    v_ref,
    in_ref,
    cot_ref,
    w_ref,
    send,
    recv,
    back,
    home,
    cot_edge,
    hid_edge,
    cot_pad,
    hid_pad,
    hidden,
    grad,
    grad_stack,
    ctx,
    ctx_stack,
    grad_picked,
    kern_grad,
    x_ref,
    parts,
    mine,
    sums,
    whole,
    load_sem,
    send_sem,
    recv_sem,
    back_sem,
    home_sem,
    edge_send,
    edge_recv,
    s1,
    r1,
    s2,
    r2,
    s3,
    r3,
):
    utts, frames, width = q_ref.shape
    taps = kern_ref.shape[0]
    lanes = PICK_TILE // 128
    held = rows_each * lanes
    reach = 16
    tokens = utts * frames
    block = width // n_seq
    head_size = width // HEADS
    me = lax.axis_index("seq")
    me_dp = lax.axis_index("dp")
    right, left = lax.rem(me + 1, n_seq), lax.rem(me + n_seq - 1, n_seq)
    loads = [
        pltpu.make_async_copy(src, dst, load_sem.at[i])
        for i, (src, dst) in enumerate(
            (
                (cot_hbm, cot_ref),
                (q_hbm, q_ref),
                (k_hbm, k_ref),
                (v_hbm, v_ref),
                (w_hbm, w_ref),
                (in_hbm, in_ref),
            )
        )
    ]
    for load in loads:
        load.start()
    greet((("seq", n_seq), ("dp", n_dp)))

    def swap_edges(rows, edge, utt, base):
        return [
            send_to(
                rows.at[utt, frames - reach : frames],
                edge.at[0, utt],
                edge_send.at[base],
                edge_recv.at[base],
                "seq",
                right,
            ),
            send_to(
                rows.at[utt, 0:reach],
                edge.at[1, utt],
                edge_send.at[base + 1],
                edge_recv.at[base + 1],
                "seq",
                left,
            ),
        ]

    def pad_edges(edge, pad):
        for utt in range(utts):
            before = edge[0, utt].astype(jnp.float32)
            after = edge[1, utt].astype(jnp.float32)
            pad[utt, 0:reach, :] = jnp.where(me > 0, before, 0.0)
            pad[utt, reach + frames : 2 * reach + frames, :] = jnp.where(
                me < n_seq - 1, after, 0.0
            )

    half = frames // 2

    def send_heads(utt):
        for owner in range(n_seq):
            for part in range(2):
                for place, ref in enumerate((q_ref, k_ref, v_ref)):
                    begin = (part * 3 + place) * block
                    send[utt, owner, :, begin : begin + block] = ref[
                        utt, part * half : (part + 1) * half, owner * block : (owner + 1) * block
                    ]
        sent = [
            send_to(
                send.at[utt, peer],
                recv.at[utt, me],
                send_sem.at[utt, i],
                recv_sem.at[utt, i],
                "seq",
                peer,
            )
            for i, peer in enumerate(peers_of("seq", n_seq))
        ]
        recv[utt, pl.ds(me, 1)] = send[utt, pl.ds(me, 1)]
        return sent

    def attend(utt):
        full = n_seq * frames
        key_ok = lax.broadcasted_iota(jnp.int32, (full, full), 1) < len_ref[utt]
        for head in range(block // head_size):
            three = []
            for place in range(3):
                pieces = []
                for part in range(2):
                    begin = (part * 3 + place) * block + head * head_size
                    pieces.append(recv[utt, :, :, begin : begin + head_size])
                three.append(jnp.concatenate(pieces, axis=1).reshape(full, head_size))
            query, key, value = three
            scores = lax.dot_general(
                query, key, (((1,), (1,)), ((), ())), preferred_element_type=jnp.float32
            )
            scores = jnp.where(key_ok, scores * score_scale, neg_big)
            probs = jnp.exp(scores - jnp.max(scores, axis=-1, keepdims=True))
            denom = jnp.sum(probs, axis=-1, keepdims=True)
            rows = jnp.dot(probs.astype(jnp.bfloat16), value, preferred_element_type=jnp.float32)
            rows = (rows / denom).astype(jnp.bfloat16).reshape(n_seq, frames, head_size)
            for part in range(2):
                begin = part * block + head * head_size
                back[utt, :, :, begin : begin + head_size] = rows[
                    :, part * half : (part + 1) * half
                ]
        sent = [
            send_to(
                back.at[utt, peer],
                home.at[utt, me],
                back_sem.at[utt, i],
                home_sem.at[utt, i],
                "seq",
                peer,
            )
            for i, peer in enumerate(peers_of("seq", n_seq))
        ]
        home[utt, pl.ds(me, 1)] = back[utt, pl.ds(me, 1)]
        return sent

    def project(utt):
        first_row = utt * frames
        for owner in range(n_seq):
            for part in range(2):
                rows = slice(first_row + part * half, first_row + (part + 1) * half)
                ctx[rows, owner * block : (owner + 1) * block] = home[
                    utt, owner, :, part * block : (part + 1) * block
                ]
        rows = slice(first_row, first_row + frames)

        @pl.loop(0, width // LOW)
        def _(step):
            cols = pl.ds(pl.multiple_of(step * LOW, LOW), LOW)
            value = jnp.dot(ctx[rows, :], w_ref[:, cols], preferred_element_type=jnp.float32)
            value = in_ref[utt, :, cols].astype(jnp.float32) + value
            value = jnp.where(frame_ids < len_ref[utt], value, 0.0).astype(jnp.bfloat16)
            hidden[utt, :, cols] = value
            hid_pad[utt, reach : reach + frames, cols] = value.astype(jnp.float32)

        sent = swap_edges(hidden, hid_edge, utt, 2 * utts + 2 * utt)
        for part in range(width // LOW):
            ctx_stack[utt, part * frames : (part + 1) * frames, :] = ctx[
                rows, part * LOW : (part + 1) * LOW
            ]
        return sent

    def pick_context(utt):
        @pl.loop(0, n_seq)
        def _(owner):
            for row in range(rows_each):
                found = choose(ctx_stack[utt], frames, lax.div(pick_row(owner, row), width))
                other = grad_picked[owner, row, utt * frames : (utt + 1) * frames, :]
                found = jnp.sum(found * other.astype(jnp.float32), axis=0, keepdims=True)
                store_row(owner, row, found, utt > 0)

    def pick_row(owner, row):
        return jnp.concatenate(
            [pick_ref[owner, lanes * row + i : lanes * row + i + 1, :] for i in range(lanes)],
            axis=1,
        )

    def store_row(owner, row, value, add):
        for i in range(lanes):
            place = slice(lanes * row + i, lanes * row + i + 1)
            piece = value[:, i * 128 : (i + 1) * 128]
            if add:
                piece = piece + x_ref[owner, place, :]
            x_ref[owner, place, :] = piece

    for load in loads[:4]:
        load.wait()
    copies = send_heads(0)
    edges = []
    for utt in range(utts):
        edges += swap_edges(cot_ref, cot_edge, utt, 2 * utt)

    frame_ids = me * frames + lax.broadcasted_iota(jnp.int32, (frames, 1), 0)
    for utt in range(utts):
        cot_pad[utt, reach : reach + frames, :] = cot_ref[utt].astype(jnp.float32)
    for copy in edges:
        copy.wait_recv()
    pad_edges(cot_edge, cot_pad)

    @pl.loop(0, width // 128)
    def _(step):
        cols = pl.ds(pl.multiple_of(step * 128, 128), 128)
        kern = kern_ref[:, cols].astype(jnp.float32)
        for utt in range(utts):
            total = jnp.zeros((frames, 128), jnp.float32)
            for offset, window in shifted_windows(cot_pad[utt, :, cols], frames):
                tap = taps - offset
                total = total + kern[tap : tap + 1] * window
            total = jnp.where(frame_ids < len_ref[utt], total, 0.0)
            grad[utt * frames : (utt + 1) * frames, cols] = total.astype(jnp.bfloat16)

    for part in range(width // LOW):
        grad_stack[part * tokens : (part + 1) * tokens, :] = grad[
            :, part * LOW : (part + 1) * LOW
        ]

    def pick_grad(begin, end):
        @pl.loop(begin, end)
        def _(owner):
            for row in range(rows_each):
                found = choose(grad_stack[...], tokens, lax.rem(pick_row(owner, row), width))
                grad_picked[owner, row] = found.astype(jnp.bfloat16)

    pick_grad(0, n_seq // 2)
    for utt in range(1, utts):
        copies += send_heads(utt)
    pick_grad(n_seq // 2, n_seq)
    returns = []
    for utt in range(utts):
        for copy in copies[utt * (n_seq - 1) : (utt + 1) * (n_seq - 1)]:
            copy.wait_recv()
        returns += attend(utt)
        if utt == 0:
            loads[4].wait()
            loads[5].wait()

            @pl.loop(0, width // LOW)
            def _(step):
                cols = pl.ds(pl.multiple_of(step * LOW, LOW), LOW)
                value = lax.dot_general(
                    grad[...],
                    w_ref[cols, :],
                    (((1,), (1,)), ((), ())),
                    preferred_element_type=jnp.float32,
                ).astype(jnp.bfloat16)
                for row in range(utts):
                    cgrad_ref[row, :, cols] = value[row * frames : (row + 1) * frames]

    hid_copies = []
    for utt in range(utts):
        for copy in returns[utt * (n_seq - 1) : (utt + 1) * (n_seq - 1)]:
            copy.wait_recv()
        hid_copies += project(utt)
        pick_context(utt)
    for copy in hid_copies:
        copy.wait_recv()
    pad_edges(hid_edge, hid_pad)
    kern_grad[...] = jnp.zeros_like(kern_grad)

    @pl.loop(0, width // 128)
    def _(step):
        cols = pl.ds(pl.multiple_of(step * 128, 128), 128)
        found = {}
        for utt in range(utts):
            cot = cot_pad[utt, reach : reach + frames, cols]
            for offset, window in shifted_windows(hid_pad[utt, :, cols], frames):
                value = jnp.sum((window * cot).reshape(frames // 8, 8, 128), axis=0)
                found[offset] = value if utt == 0 else found[offset] + value
        for offset, value in found.items():
            kern_grad[offset - 1 : offset, cols] = jnp.sum(value, axis=0, keepdims=True)

    pick = pick_row(n_seq - 1, rows_each - 1)
    rest = jnp.concatenate(
        [kern_grad[:, part * LOW : (part + 1) * LOW] for part in range(width // LOW)], axis=0
    )
    found = jnp.zeros((kern_grad.shape[0], PICK_TILE), jnp.float32)
    for _ in range(3):
        piece = rest.astype(jnp.bfloat16)
        rest = rest - piece.astype(jnp.float32)
        found = found + choose(piece, kern_grad.shape[0], lax.rem(pick, width))
    tap_ids = lax.broadcasted_iota(jnp.int32, found.shape, 0)
    found = jnp.where(tap_ids == lax.div(pick, width), found, 0.0)
    store_row(n_seq - 1, rows_each - 1, jnp.sum(found, axis=0, keepdims=True), False)

    first = [
        send_to(x_ref.at[peer], parts.at[me], s1.at[i], r1.at[i], "seq", peer)
        for i, peer in enumerate(peers_of("seq", n_seq))
    ]
    parts[pl.ds(me, 1)] = x_ref[pl.ds(me, 1)]

    def convolve(begin, end):
        @pl.loop(begin, end)
        def _(step):
            cols = pl.ds(pl.multiple_of(step * 128, 128), 128)
            kern = kern_ref[:, cols].astype(jnp.float32)
            for utt in range(utts):
                total = jnp.zeros((frames, 128), jnp.float32)
                for offset, window in shifted_windows(hid_pad[utt, :, cols], frames):
                    total = total + kern[offset - 1 : offset] * window
                conv_ref[utt, :, cols] = total.astype(jnp.bfloat16)

    third_part = width // 128 // 3
    convolve(0, third_part)
    for copy in first:
        copy.wait_recv()
    mine[...] = jnp.sum(parts[...], axis=0)
    second = [
        send_to(mine, sums.at[me_dp], s2.at[i], r2.at[i], "dp", peer)
        for i, peer in enumerate(peers_of("dp", n_dp))
    ]
    sums[pl.ds(me_dp, 1)] = mine[...][None]
    convolve(third_part, 2 * third_part)
    for copy in second:
        copy.wait_recv()
    whole[pl.ds(me, 1)] = (jnp.sum(sums[...], axis=0) * norm_factor)[None]
    third = [
        send_to(whole.at[me], whole.at[me], s3.at[i], r3.at[i], "seq", peer)
        for i, peer in enumerate(peers_of("seq", n_seq))
    ]
    convolve(2 * third_part, width // 128)
    for copy in third:
        copy.wait_recv()
    for owner in range(n_seq):
        sum_ref[owner * held : (owner + 1) * held] = whole[owner]
    for copy in edges + copies + returns + hid_copies + first + second + third:
        copy.wait_send()


def write_kernel(*refs):
    count = len(refs) // 2
    sems = refs[-1]
    copies = [
        pltpu.make_async_copy(refs[i], refs[count + i], sems.at[i]) for i in range(count)
    ]
    for copy in copies:
        copy.start()
    for copy in copies:
        copy.wait()


def written(*arrays):
    spec = pl.BlockSpec(memory_space=pl.ANY)
    return pl.pallas_call(
        write_kernel,
        out_shape=[jax.ShapeDtypeStruct(array.shape, array.dtype) for array in arrays],
        in_specs=[spec] * len(arrays),
        out_specs=[spec] * len(arrays),
        scratch_shapes=[pltpu.SemaphoreType.DMA((len(arrays),))],
        compiler_params=pltpu.CompilerParams(vmem_limit_bytes=56 * 2**20),
    )(*arrays)


def one_kernel(
    queries,
    key_rows,
    value_rows,
    layer_input,
    utt_lengths,
    out_weight,
    conv_kernel,
    conv_cotangent,
    pick_weight,
    pick_kernel,
):
    utts, frames, width = queries.shape
    n_seq, n_dp = lax.axis_size("seq"), lax.axis_size("dp")
    block = width // n_seq
    tokens = utts * frames
    tiles = -(-pick_weight.shape[0] // PICK_TILE) + 1
    rows_each = -(-tiles // (2 * n_seq)) * 2
    held_rows = rows_each * PICK_TILE // 128
    kernel_start = (rows_each * n_seq - 1) * PICK_TILE
    picks = jnp.concatenate(
        [
            jnp.pad(pick_weight, (0, kernel_start - pick_weight.shape[0])),
            jnp.pad(pick_kernel, (0, PICK_TILE - pick_kernel.shape[0])),
        ]
    ).reshape(n_seq, held_rows, 128)
    vmem = pl.BlockSpec(memory_space=pltpu.VMEM)
    hbm = pl.BlockSpec(memory_space=pl.ANY)
    bf16, f32 = jnp.bfloat16, jnp.float32
    local = pltpu.VMEM((utts, frames, width), bf16)
    wide = pltpu.VMEM((utts, n_seq, frames // 2, 6 * block), bf16)
    narrow = pltpu.VMEM((utts, n_seq, frames // 2, 2 * block), bf16)
    edge = pltpu.VMEM((2, utts, 16, width), bf16)
    pad = pltpu.VMEM((utts, frames + 32, width), f32)
    flat = pltpu.VMEM((tokens, width), bf16)
    stack = pltpu.VMEM((tokens * width // LOW, LOW), bf16)
    partial = pltpu.VMEM((n_seq, held_rows, 128), f32)
    seq_sems = pltpu.SemaphoreType.DMA((n_seq - 1,))
    dp_sems = pltpu.SemaphoreType.DMA((n_dp - 1,))
    utt_sems = pltpu.SemaphoreType.DMA((utts, n_seq - 1))
    score_scale = 1.0 / math.sqrt(width // HEADS)
    norm_factor = 1.0 / math.sqrt(utts * n_dp * frames * n_seq)
    conv_out, context_grad, total = pl.pallas_call(
        functools.partial(block_kernel, n_seq, n_dp, rows_each, score_scale, norm_factor),
        out_shape=(
            jax.ShapeDtypeStruct(queries.shape, bf16),
            jax.ShapeDtypeStruct(queries.shape, bf16),
            jax.ShapeDtypeStruct((n_seq * held_rows, 128), f32),
        ),
        in_specs=[pl.BlockSpec(memory_space=pltpu.SMEM), vmem, vmem] + [hbm] * 6,
        out_specs=(vmem, vmem, vmem),
        scratch_shapes=[
            local,
            local,
            local,
            local,
            local,
            pltpu.VMEM((width, width), bf16),
            wide,
            wide,
            narrow,
            narrow,
            edge,
            edge,
            pad,
            pad,
            local,
            flat,
            stack,
            flat,
            pltpu.VMEM((utts, frames * width // LOW, LOW), bf16),
            pltpu.VMEM((n_seq, rows_each, tokens, PICK_TILE), bf16),
            pltpu.VMEM((32, width), f32),
            partial,
            partial,
            pltpu.VMEM((held_rows, 128), f32),
            pltpu.VMEM((n_dp, held_rows, 128), f32),
            partial,
            pltpu.SemaphoreType.DMA((6,)),
            utt_sems,
            utt_sems,
            utt_sems,
            utt_sems,
            pltpu.SemaphoreType.DMA((4 * utts,)),
            pltpu.SemaphoreType.DMA((4 * utts,)),
            seq_sems,
            seq_sems,
            dp_sems,
            dp_sems,
            seq_sems,
            seq_sems,
        ],
        compiler_params=pltpu.CompilerParams(
            collective_id=2, has_side_effects=True, vmem_limit_bytes=56 * 2**20
        ),
    )(
        utt_lengths,
        picks,
        conv_kernel,
        queries,
        key_rows,
        value_rows,
        layer_input,
        conv_cotangent,
        out_weight,
    )
    conv_out, context_grad, total = written(conv_out, context_grad, total)
    flat_total = total.reshape(-1)
    weight_picks = flat_total[: pick_weight.shape[0]]
    kernel_picks = flat_total[kernel_start : kernel_start + pick_kernel.shape[0]]
    return (conv_out, context_grad, weight_picks, kernel_picks)


def on_device(
    queries,
    key_rows,
    value_rows,
    layer_input,
    utt_lengths,
    out_weight,
    conv_kernel,
    conv_cotangent,
    pick_weight,
    pick_kernel,
):
    local_utts, frames_dev, width = queries.shape
    seq_count = lax.axis_size("seq")
    if HEADS % seq_count == 0:
        return one_kernel(
            queries,
            key_rows,
            value_rows,
            layer_input,
            utt_lengths,
            out_weight,
            conv_kernel,
            conv_cotangent,
            pick_weight,
            pick_kernel,
        )
    full_frames = frames_dev * seq_count
    head_size = width // HEADS
    score_scale = 1.0 / math.sqrt(head_size)
    first_frame = lax.axis_index("seq") * frames_dev
    local_ids = first_frame + jnp.arange(frames_dev, dtype=jnp.int32)
    valid_rows = (local_ids[None, :] < utt_lengths[:, None]).astype(jnp.float32)
    context = gathered_attention(queries, key_rows, value_rows, utt_lengths, score_scale)
    context_flat = context.reshape(local_utts * frames_dev, width)
    projected = jnp.dot(context_flat, out_weight, preferred_element_type=jnp.float32).reshape(
        local_utts, frames_dev, width
    )
    hidden = ((layer_input.astype(jnp.float32) + projected) * valid_rows[:, :, None]).astype(
        jnp.bfloat16
    )
    tap_count = conv_kernel.shape[0]
    half_taps = (tap_count - 1) // 2
    kernel_f = conv_kernel.astype(jnp.float32)
    hidden_pad = padded(hidden, (("seq", 1),), half_taps)
    cot_f = conv_cotangent.astype(jnp.float32)
    conv_sum = jnp.zeros((local_utts, frames_dev, width), jnp.float32)
    kernel_rows = []
    for offset in range(tap_count):
        window = hidden_pad[:, offset : offset + frames_dev].astype(jnp.float32)
        conv_sum = conv_sum + kernel_f[offset] * window
        kernel_rows.append(jnp.sum(window * cot_f, axis=(0, 1)))
    conv_out = conv_sum.astype(jnp.bfloat16)
    kernel_grad = jnp.stack(kernel_rows)
    cot_pad = padded(conv_cotangent, (("seq", 1),), half_taps).astype(jnp.float32)
    back_sum = jnp.zeros((local_utts, frames_dev, width), jnp.float32)
    for offset in range(tap_count):
        begin = 2 * half_taps - offset
        back_sum = back_sum + kernel_f[offset] * cot_pad[:, begin : begin + frames_dev]
    hidden_grad = (back_sum * valid_rows[:, :, None]).astype(jnp.bfloat16)
    grad_flat = hidden_grad.reshape(local_utts * frames_dev, width)
    context_grad = lax.dot_general(
        grad_flat, out_weight, (((1,), (1,)), ((), ())), preferred_element_type=jnp.float32
    )
    context_grad = context_grad.reshape(local_utts, frames_dev, width).astype(jnp.bfloat16)
    weight_vals = picked_products(context_flat, grad_flat, pick_weight)
    kernel_vals = pick_entries(kernel_grad, pick_kernel)
    total = summed(jnp.concatenate([weight_vals, kernel_vals]))
    weight_sum = total[: pick_weight.shape[0]]
    kernel_sum = total[weight_vals.shape[0] : weight_vals.shape[0] + pick_kernel.shape[0]]
    total_slots = local_utts * lax.axis_size("dp") * full_frames
    norm_factor = 1.0 / math.sqrt(total_slots)
    return (conv_out, context_grad, weight_sum * norm_factor, kernel_sum * norm_factor)


def solution(mesh):
    placed = (
        P("dp", "seq", None),
        P("dp", "seq", None),
        P("dp", "seq", None),
        P("dp", "seq", None),
        P("dp"),
        P(),
        P(),
        P("dp", "seq", None),
        P(),
        P(),
    )
    return jax.shard_map(
        on_device,
        mesh=mesh,
        in_specs=placed,
        out_specs=(P("dp", "seq", None), P("dp", "seq", None), P(), P()),
        check_vma=False,
    )
```

```python
import functools
import math

import jax
import jax.numpy as jnp
from jax import lax
from jax.experimental import pallas as pl
from jax.experimental.pallas import tpu as pltpu
from jax.sharding import PartitionSpec as P

HEADS = 16


neg_big = -1e30


def padded(value, sides, width):
    for axis, dim in sides:
        count, length = (lax.axis_size(axis), value.shape[dim])
        up = [(i, (i + 1) % count) for i in range(count - 1)]
        down = [(j, i) for i, j in up]
        last = lax.slice_in_dim(value, length - width, length, axis=dim)
        leading = lax.slice_in_dim(value, 0, width, axis=dim)
        before = lax.ppermute(last, axis, up)
        after = lax.ppermute(leading, axis, down)
        value = jnp.concatenate([before, value, after], axis=dim)
    return value


def softmax_rows(scores, key_ok):
    scores = jnp.where(key_ok, scores, neg_big)
    row_max = jnp.max(scores, axis=-1, keepdims=True)
    probs = jnp.exp(scores - row_max)
    return (probs.astype(jnp.bfloat16), jnp.sum(probs, axis=-1))


def pick_entries(table, picks):
    flat = table.reshape(-1)
    lane = math.gcd(flat.shape[0], 128)
    blocks = flat.reshape(flat.shape[0] // lane, lane)
    chosen = jnp.take(blocks, picks // lane, axis=0)
    lane_ids = jnp.arange(lane, dtype=jnp.int32)
    hit = lane_ids[None, :] == (picks % lane)[:, None]
    return jnp.sum(jnp.where(hit, chosen, jnp.float32(0.0)), axis=1)


def peers_of(axis, count):
    me = lax.axis_index(axis)
    return [lax.rem(me + step, count) for step in range(1, count)]


def greet(axes):
    barrier = pltpu.get_barrier_semaphore()
    total = 0
    for axis, count in axes:
        for peer in peers_of(axis, count):
            pl.semaphore_signal(
                barrier, inc=1, device_id={axis: peer}, device_id_type=pl.DeviceIdType.MESH
            )
            total += 1
    pl.semaphore_wait(barrier, total)


def send_to(src, dst, send_sem, recv_sem, axis, peer):
    copy = pltpu.make_async_remote_copy(
        src_ref=src,
        dst_ref=dst,
        send_sem=send_sem,
        recv_sem=recv_sem,
        device_id={axis: peer},
        device_id_type=pl.DeviceIdType.MESH,
    )
    copy.start()
    return copy


def total_kernel(
    n_seq, n_dp, x_ref, out_ref, parts, mine, sums, whole, s1, r1, s2, r2, s3, r3
):
    me = lax.axis_index("seq")
    me_dp = lax.axis_index("dp")
    greet((("seq", n_seq), ("dp", n_dp)))
    copies = [
        send_to(x_ref.at[peer], parts.at[me], s1.at[i], r1.at[i], "seq", peer)
        for i, peer in enumerate(peers_of("seq", n_seq))
    ]
    parts[pl.ds(me, 1)] = x_ref[pl.ds(me, 1)]
    for copy in copies:
        copy.wait_recv()
    mine[...] = jnp.sum(parts[...], axis=0)
    second = [
        send_to(mine, sums.at[me_dp], s2.at[i], r2.at[i], "dp", peer)
        for i, peer in enumerate(peers_of("dp", n_dp))
    ]
    sums[pl.ds(me_dp, 1)] = mine[...][None]
    for copy in second:
        copy.wait_recv()
    whole[pl.ds(me, 1)] = jnp.sum(sums[...], axis=0)[None]
    third = [
        send_to(whole.at[me], whole.at[me], s3.at[i], r3.at[i], "seq", peer)
        for i, peer in enumerate(peers_of("seq", n_seq))
    ]
    for copy in third:
        copy.wait_recv()
    out_ref[...] = whole[...]
    for copy in copies + second + third:
        copy.wait_send()


def summed(values):
    n_seq, n_dp = lax.axis_size("seq"), lax.axis_size("dp")
    chunk = 128 * 8 * n_seq
    rows = -(-values.shape[0] // chunk) * 8
    x = jnp.pad(values, (0, rows * 128 * n_seq - values.shape[0])).reshape(n_seq, rows, 128)
    vmem = pl.BlockSpec(memory_space=pltpu.VMEM)
    seq_sems = pltpu.SemaphoreType.DMA((n_seq - 1,))
    dp_sems = pltpu.SemaphoreType.DMA((n_dp - 1,))
    out = pl.pallas_call(
        functools.partial(total_kernel, n_seq, n_dp),
        out_shape=jax.ShapeDtypeStruct(x.shape, jnp.float32),
        in_specs=[vmem],
        out_specs=vmem,
        scratch_shapes=[
            pltpu.VMEM(x.shape, jnp.float32),
            pltpu.VMEM((rows, 128), jnp.float32),
            pltpu.VMEM((n_dp, rows, 128), jnp.float32),
            pltpu.VMEM(x.shape, jnp.float32),
            seq_sems,
            seq_sems,
            dp_sems,
            dp_sems,
            seq_sems,
            seq_sems,
        ],
        compiler_params=pltpu.CompilerParams(collective_id=1, has_side_effects=True),
    )(x)
    return out.reshape(-1)


LOW = 256
PICK_TILE = 512


def choose(stacked, tokens, index):
    low = lax.rem(index, LOW)
    high = lax.div(index, LOW)
    ids = lax.broadcasted_iota(jnp.int32, (LOW, index.shape[1]), 0).astype(jnp.bfloat16)
    one, zero = jnp.bfloat16(1.0), jnp.bfloat16(0.0)
    hot = jnp.where(ids == low.astype(jnp.bfloat16), one, zero)
    every = jnp.dot(stacked, hot, preferred_element_type=jnp.float32)
    out = every[:tokens]
    for part in range(1, stacked.shape[0] // tokens):
        out = jnp.where(high == part, every[part * tokens : (part + 1) * tokens], out)
    return out


def picks_kernel(pick_ref, ctx_ref, grad_ref, out_ref, ctx_stack, grad_stack):
    tokens, width = ctx_ref.shape

    @pl.when(pl.program_id(0) == 0)
    def _():
        for part in range(width // LOW):
            cols = slice(part * LOW, (part + 1) * LOW)
            rows = slice(part * tokens, (part + 1) * tokens)
            ctx_stack[rows, :] = ctx_ref[:, cols]
            grad_stack[rows, :] = grad_ref[:, cols]

    pick = pick_ref[...]
    left = choose(ctx_stack[...], tokens, lax.div(pick, width))
    right = choose(grad_stack[...], tokens, lax.rem(pick, width))
    out_ref[...] = jnp.sum(left * right, axis=0, keepdims=True)


def picked_products(ctx, grad, picks):
    tokens, width = ctx.shape
    steps = -(-picks.shape[0] // PICK_TILE)
    padded_picks = jnp.pad(picks, (0, steps * PICK_TILE - picks.shape[0])).reshape(1, -1)
    whole = pl.BlockSpec((tokens, width), lambda i: (0, 0))
    tile = pl.BlockSpec((1, PICK_TILE), lambda i: (0, i))
    stack = pltpu.VMEM((tokens * width // LOW, LOW), jnp.bfloat16)
    out = pl.pallas_call(
        picks_kernel,
        grid=(steps,),
        out_shape=jax.ShapeDtypeStruct(padded_picks.shape, jnp.float32),
        in_specs=[tile, whole, whole],
        out_specs=tile,
        scratch_shapes=[stack, stack],
        compiler_params=pltpu.CompilerParams(vmem_limit_bytes=40 * 2**20),
    )(padded_picks, ctx, grad)
    return out.reshape(-1)


def gathered_attention(queries, key_rows, value_rows, utt_lengths, score_scale):
    local_utts, frames_dev, width = queries.shape
    full_frames = frames_dev * lax.axis_size("seq")
    head_size = width // HEADS
    all_keys, all_values = (
        lax.all_gather(key_rows, "seq", axis=1, tiled=True),
        lax.all_gather(value_rows, "seq", axis=1, tiled=True),
    )
    full_ids = jnp.arange(full_frames, dtype=jnp.int32)

    def one_utt(item):
        query_utt, key_utt, value_utt, length_utt = item
        query_heads = query_utt.reshape(frames_dev, HEADS, head_size)
        key_heads = key_utt.reshape(full_frames, HEADS, head_size)
        value_heads = value_utt.reshape(full_frames, HEADS, head_size)
        scores = (
            jnp.einsum("qhd,khd->hqk", query_heads, key_heads, preferred_element_type=jnp.float32)
            * score_scale
        )
        weights, denom = softmax_rows(scores, (full_ids < length_utt)[None, None, :])
        out_rows = jnp.einsum(
            "hqk,khd->qhd", weights, value_heads, preferred_element_type=jnp.float32
        )
        out_rows = out_rows / denom.transpose(1, 0)[:, :, None]
        return out_rows.astype(jnp.bfloat16).reshape(frames_dev, width)

    return lax.map(one_utt, (queries, all_keys, all_values, utt_lengths))


def shifted_windows(chunk, frames):
    for turn in range(8):
        part = chunk[turn : turn + frames + 24]
        for eight in range(4):
            offset = 8 * eight + turn
            if 1 <= offset <= 31:
                yield offset, part[8 * eight : 8 * eight + frames]


def block_kernel(
    n_seq,
    n_dp,
    rows_each,
    score_scale,
    norm_factor,
    len_ref,
    pick_ref,
    kern_ref,
    q_hbm,
    k_hbm,
    v_hbm,
    in_hbm,
    cot_hbm,
    w_hbm,
    conv_ref,
    cgrad_ref,
    sum_ref,
    tile_ref,
    q_ref,
    k_ref,
    v_ref,
    in_ref,
    cot_ref,
    w_ref,
    send,
    recv,
    back,
    home,
    cot_edge,
    hid_edge,
    cot_pad,
    hid_pad,
    hidden,
    grad,
    grad_stack,
    ctx,
    ctx_stack,
    grad_picked,
    kern_grad,
    x_ref,
    parts,
    mine,
    sums,
    whole,
    tile,
    tile_parts,
    tile_mine,
    tile_sums,
    load_sem,
    send_sem,
    recv_sem,
    back_sem,
    home_sem,
    edge_send,
    edge_recv,
    s1,
    r1,
    s2,
    r2,
    s3,
    r3,
    s4,
    r4,
    s5,
    r5,
):
    utts, frames, width = q_ref.shape
    taps = kern_ref.shape[0]
    lanes = PICK_TILE // 128
    held = rows_each * lanes
    reach = 16
    tokens = utts * frames
    block = width // n_seq
    head_size = width // HEADS
    me = lax.axis_index("seq")
    me_dp = lax.axis_index("dp")
    right, left = lax.rem(me + 1, n_seq), lax.rem(me + n_seq - 1, n_seq)
    loads = [
        pltpu.make_async_copy(src, dst, load_sem.at[i])
        for i, (src, dst) in enumerate(
            (
                (cot_hbm, cot_ref),
                (q_hbm, q_ref),
                (k_hbm, k_ref),
                (v_hbm, v_ref),
                (w_hbm, w_ref),
                (in_hbm, in_ref),
            )
        )
    ]
    for load in loads:
        load.start()
    greet((("seq", n_seq), ("dp", n_dp)))

    def swap_edges(rows, edge, utt, base):
        return [
            send_to(
                rows.at[utt, frames - reach : frames],
                edge.at[0, utt],
                edge_send.at[base],
                edge_recv.at[base],
                "seq",
                right,
            ),
            send_to(
                rows.at[utt, 0:reach],
                edge.at[1, utt],
                edge_send.at[base + 1],
                edge_recv.at[base + 1],
                "seq",
                left,
            ),
        ]

    def pad_edges(edge, pad):
        for utt in range(utts):
            before = edge[0, utt].astype(jnp.float32)
            after = edge[1, utt].astype(jnp.float32)
            pad[utt, 0:reach, :] = jnp.where(me > 0, before, 0.0)
            pad[utt, reach + frames : 2 * reach + frames, :] = jnp.where(
                me < n_seq - 1, after, 0.0
            )

    half = frames // 2

    def send_heads(utt):
        for owner in range(n_seq):
            for part in range(2):
                for place, ref in enumerate((q_ref, k_ref, v_ref)):
                    begin = (part * 3 + place) * block
                    send[utt, owner, :, begin : begin + block] = ref[
                        utt, part * half : (part + 1) * half, owner * block : (owner + 1) * block
                    ]
        sent = [
            send_to(
                send.at[utt, peer],
                recv.at[utt, me],
                send_sem.at[utt, i],
                recv_sem.at[utt, i],
                "seq",
                peer,
            )
            for i, peer in enumerate(peers_of("seq", n_seq))
        ]
        recv[utt, pl.ds(me, 1)] = send[utt, pl.ds(me, 1)]
        return sent

    def attend(utt):
        full = n_seq * frames
        key_ok = lax.broadcasted_iota(jnp.int32, (full, full), 1) < len_ref[utt]
        for head in range(block // head_size):
            three = []
            for place in range(3):
                pieces = []
                for part in range(2):
                    begin = (part * 3 + place) * block + head * head_size
                    pieces.append(recv[utt, :, :, begin : begin + head_size])
                three.append(jnp.concatenate(pieces, axis=1).reshape(full, head_size))
            query, key, value = three
            scores = lax.dot_general(
                query, key, (((1,), (1,)), ((), ())), preferred_element_type=jnp.float32
            )
            scores = jnp.where(key_ok, scores * score_scale, neg_big)
            probs = jnp.exp(scores - jnp.max(scores, axis=-1, keepdims=True))
            denom = jnp.sum(probs, axis=-1, keepdims=True)
            rows = jnp.dot(probs.astype(jnp.bfloat16), value, preferred_element_type=jnp.float32)
            rows = (rows / denom).astype(jnp.bfloat16).reshape(n_seq, frames, head_size)
            for part in range(2):
                begin = part * block + head * head_size
                back[utt, :, :, begin : begin + head_size] = rows[
                    :, part * half : (part + 1) * half
                ]
        sent = [
            send_to(
                back.at[utt, peer],
                home.at[utt, me],
                back_sem.at[utt, i],
                home_sem.at[utt, i],
                "seq",
                peer,
            )
            for i, peer in enumerate(peers_of("seq", n_seq))
        ]
        home[utt, pl.ds(me, 1)] = back[utt, pl.ds(me, 1)]
        return sent

    def project(utt):
        first_row = utt * frames
        for owner in range(n_seq):
            for part in range(2):
                rows = slice(first_row + part * half, first_row + (part + 1) * half)
                ctx[rows, owner * block : (owner + 1) * block] = home[
                    utt, owner, :, part * block : (part + 1) * block
                ]
        rows = slice(first_row, first_row + frames)

        @pl.loop(0, width // LOW)
        def _(step):
            cols = pl.ds(pl.multiple_of(step * LOW, LOW), LOW)
            value = jnp.dot(ctx[rows, :], w_ref[:, cols], preferred_element_type=jnp.float32)
            value = in_ref[utt, :, cols].astype(jnp.float32) + value
            value = jnp.where(frame_ids < len_ref[utt], value, 0.0).astype(jnp.bfloat16)
            hidden[utt, :, cols] = value
            hid_pad[utt, reach : reach + frames, cols] = value.astype(jnp.float32)

        sent = swap_edges(hidden, hid_edge, utt, 2 * utts + 2 * utt)
        for part in range(width // LOW):
            begin = part * tokens + first_row
            ctx_stack[begin : begin + frames, :] = ctx[rows, part * LOW : (part + 1) * LOW]
        return sent

    def pick_context():
        @pl.loop(0, n_seq)
        def _(owner):
            for row in range(rows_each):
                found = choose(ctx_stack[...], tokens, lax.div(pick_row(owner, row), width))
                found = found * grad_picked[owner, row].astype(jnp.float32)
                store_row(x_ref.at[owner], row, jnp.sum(found, axis=0, keepdims=True))

    def pick_row(owner, row):
        return jnp.concatenate(
            [pick_ref[owner, lanes * row + i : lanes * row + i + 1, :] for i in range(lanes)],
            axis=1,
        )

    def store_row(ref, row, value):
        for i in range(lanes):
            place = slice(lanes * row + i, lanes * row + i + 1)
            ref[place, :] = value[:, i * 128 : (i + 1) * 128]

    for load in loads[:4]:
        load.wait()
    copies = send_heads(0)
    edges = []
    for utt in range(utts):
        edges += swap_edges(cot_ref, cot_edge, utt, 2 * utt)

    frame_ids = me * frames + lax.broadcasted_iota(jnp.int32, (frames, 1), 0)
    for utt in range(utts):
        cot_pad[utt, reach : reach + frames, :] = cot_ref[utt].astype(jnp.float32)
    for copy in edges:
        copy.wait_recv()
    pad_edges(cot_edge, cot_pad)

    @pl.loop(0, width // 128)
    def _(step):
        cols = pl.ds(pl.multiple_of(step * 128, 128), 128)
        kern = kern_ref[:, cols].astype(jnp.float32)
        for utt in range(utts):
            total = jnp.zeros((frames, 128), jnp.float32)
            for offset, window in shifted_windows(cot_pad[utt, :, cols], frames):
                tap = taps - offset
                total = total + kern[tap : tap + 1] * window
            total = jnp.where(frame_ids < len_ref[utt], total, 0.0)
            grad[utt * frames : (utt + 1) * frames, cols] = total.astype(jnp.bfloat16)

    for part in range(width // LOW):
        grad_stack[part * tokens : (part + 1) * tokens, :] = grad[
            :, part * LOW : (part + 1) * LOW
        ]

    def pick_grad(begin, end):
        @pl.loop(begin, end)
        def _(owner):
            for row in range(rows_each):
                found = choose(grad_stack[...], tokens, lax.rem(pick_row(owner, row), width))
                grad_picked[owner, row] = found.astype(jnp.bfloat16)

    for utt in range(1, utts):
        copies += send_heads(utt)
    pick_grad(0, n_seq)
    returns = []
    for utt in range(utts):
        for copy in copies[utt * (n_seq - 1) : (utt + 1) * (n_seq - 1)]:
            copy.wait_recv()
        returns += attend(utt)
    loads[4].wait()
    loads[5].wait()

    @pl.loop(0, width // LOW)
    def _(step):
        cols = pl.ds(pl.multiple_of(step * LOW, LOW), LOW)
        value = lax.dot_general(
            grad[...], w_ref[cols, :], (((1,), (1,)), ((), ())), preferred_element_type=jnp.float32
        ).astype(jnp.bfloat16)
        for row in range(utts):
            cgrad_ref[row, :, cols] = value[row * frames : (row + 1) * frames]

    hid_copies = []
    for utt in range(utts):
        for copy in returns[utt * (n_seq - 1) : (utt + 1) * (n_seq - 1)]:
            copy.wait_recv()
        hid_copies += project(utt)
    pick_context()
    first = [
        send_to(x_ref.at[peer], parts.at[me], s1.at[i], r1.at[i], "seq", peer)
        for i, peer in enumerate(peers_of("seq", n_seq))
    ]
    parts[pl.ds(me, 1)] = x_ref[pl.ds(me, 1)]
    for copy in hid_copies:
        copy.wait_recv()
    pad_edges(hid_edge, hid_pad)
    kern_grad[...] = jnp.zeros_like(kern_grad)

    @pl.loop(0, width // 128)
    def _(step):
        cols = pl.ds(pl.multiple_of(step * 128, 128), 128)
        found = {}
        for utt in range(utts):
            cot = cot_pad[utt, reach : reach + frames, cols]
            for offset, window in shifted_windows(hid_pad[utt, :, cols], frames):
                value = jnp.sum((window * cot).reshape(frames // 8, 8, 128), axis=0)
                found[offset] = value if utt == 0 else found[offset] + value
        for offset, value in found.items():
            kern_grad[offset - 1 : offset, cols] = jnp.sum(value, axis=0, keepdims=True)

    pick = pick_row(n_seq - 1, rows_each - 1)
    rest = jnp.concatenate(
        [kern_grad[:, part * LOW : (part + 1) * LOW] for part in range(width // LOW)], axis=0
    )
    found = jnp.zeros((kern_grad.shape[0], PICK_TILE), jnp.float32)
    for _ in range(3):
        piece = rest.astype(jnp.bfloat16)
        rest = rest - piece.astype(jnp.float32)
        found = found + choose(piece, kern_grad.shape[0], lax.rem(pick, width))
    tap_ids = lax.broadcasted_iota(jnp.int32, found.shape, 0)
    found = jnp.where(tap_ids == lax.div(pick, width), found, 0.0)
    tile[...] = jnp.zeros_like(tile)
    store_row(tile, 0, jnp.sum(found, axis=0, keepdims=True))

    tile_first = [
        send_to(tile, tile_parts.at[me], s4.at[i], r4.at[i], "seq", peer)
        for i, peer in enumerate(peers_of("seq", n_seq))
    ]
    tile_parts[pl.ds(me, 1)] = tile[...][None]

    def convolve(begin, end):
        @pl.loop(begin, end)
        def _(step):
            cols = pl.ds(pl.multiple_of(step * 128, 128), 128)
            kern = kern_ref[:, cols].astype(jnp.float32)
            for utt in range(utts):
                total = jnp.zeros((frames, 128), jnp.float32)
                for offset, window in shifted_windows(hid_pad[utt, :, cols], frames):
                    total = total + kern[offset - 1 : offset] * window
                conv_ref[utt, :, cols] = total.astype(jnp.bfloat16)

    third_part = width // 128 // 3
    for copy in first:
        copy.wait_recv()
    mine[...] = jnp.sum(parts[...], axis=0)
    second = [
        send_to(mine, sums.at[me_dp], s2.at[i], r2.at[i], "dp", peer)
        for i, peer in enumerate(peers_of("dp", n_dp))
    ]
    sums[pl.ds(me_dp, 1)] = mine[...][None]
    convolve(0, third_part)
    for copy in tile_first:
        copy.wait_recv()
    tile_mine[...] = jnp.sum(tile_parts[...], axis=0)
    tile_second = [
        send_to(tile_mine, tile_sums.at[me_dp], s5.at[i], r5.at[i], "dp", peer)
        for i, peer in enumerate(peers_of("dp", n_dp))
    ]
    tile_sums[pl.ds(me_dp, 1)] = tile_mine[...][None]
    for copy in second:
        copy.wait_recv()
    whole[pl.ds(me, 1)] = (jnp.sum(sums[...], axis=0) * norm_factor)[None]
    third = [
        send_to(whole.at[me], whole.at[me], s3.at[i], r3.at[i], "seq", peer)
        for i, peer in enumerate(peers_of("seq", n_seq))
    ]
    convolve(third_part, width // 128)
    for copy in tile_second:
        copy.wait_recv()
    tile_ref[...] = jnp.sum(tile_sums[...], axis=0) * norm_factor
    for copy in third:
        copy.wait_recv()
    for owner in range(n_seq):
        sum_ref[owner * held : (owner + 1) * held] = whole[owner]
    for copy in edges + copies + returns + hid_copies + first + second + third:
        copy.wait_send()
    for copy in tile_first + tile_second:
        copy.wait_send()


def one_kernel(
    queries,
    key_rows,
    value_rows,
    layer_input,
    utt_lengths,
    out_weight,
    conv_kernel,
    conv_cotangent,
    pick_weight,
    pick_kernel,
):
    utts, frames, width = queries.shape
    n_seq, n_dp = lax.axis_size("seq"), lax.axis_size("dp")
    block = width // n_seq
    tokens = utts * frames
    tiles = -(-pick_weight.shape[0] // PICK_TILE) + 1
    rows_each = -(-tiles // (2 * n_seq)) * 2
    held_rows = rows_each * PICK_TILE // 128
    kernel_start = (rows_each * n_seq - 1) * PICK_TILE
    picks = jnp.concatenate(
        [
            jnp.pad(pick_weight, (0, kernel_start - pick_weight.shape[0])),
            jnp.pad(pick_kernel, (0, PICK_TILE - pick_kernel.shape[0])),
        ]
    ).reshape(n_seq, held_rows, 128)
    vmem = pl.BlockSpec(memory_space=pltpu.VMEM)
    hbm = pl.BlockSpec(memory_space=pl.ANY)
    bf16, f32 = jnp.bfloat16, jnp.float32
    local = pltpu.VMEM((utts, frames, width), bf16)
    wide = pltpu.VMEM((utts, n_seq, frames // 2, 6 * block), bf16)
    narrow = pltpu.VMEM((utts, n_seq, frames // 2, 2 * block), bf16)
    edge = pltpu.VMEM((2, utts, 16, width), bf16)
    pad = pltpu.VMEM((utts, frames + 32, width), f32)
    flat = pltpu.VMEM((tokens, width), bf16)
    stack = pltpu.VMEM((tokens * width // LOW, LOW), bf16)
    partial = pltpu.VMEM((n_seq, held_rows, 128), f32)
    seq_sems = pltpu.SemaphoreType.DMA((n_seq - 1,))
    dp_sems = pltpu.SemaphoreType.DMA((n_dp - 1,))
    utt_sems = pltpu.SemaphoreType.DMA((utts, n_seq - 1))
    score_scale = 1.0 / math.sqrt(width // HEADS)
    norm_factor = 1.0 / math.sqrt(utts * n_dp * frames * n_seq)
    conv_out, context_grad, total, tile = pl.pallas_call(
        functools.partial(block_kernel, n_seq, n_dp, rows_each, score_scale, norm_factor),
        out_shape=(
            jax.ShapeDtypeStruct(queries.shape, bf16),
            jax.ShapeDtypeStruct(queries.shape, bf16),
            jax.ShapeDtypeStruct((n_seq * held_rows, 128), f32),
            jax.ShapeDtypeStruct((8, 128), f32),
        ),
        in_specs=[pl.BlockSpec(memory_space=pltpu.SMEM), vmem, vmem] + [hbm] * 6,
        out_specs=(vmem, vmem, vmem, vmem),
        scratch_shapes=[
            local,
            local,
            local,
            local,
            local,
            pltpu.VMEM((width, width), bf16),
            wide,
            wide,
            narrow,
            narrow,
            edge,
            edge,
            pad,
            pad,
            local,
            flat,
            stack,
            flat,
            stack,
            pltpu.VMEM((n_seq, rows_each, tokens, PICK_TILE), bf16),
            pltpu.VMEM((32, width), f32),
            partial,
            partial,
            pltpu.VMEM((held_rows, 128), f32),
            pltpu.VMEM((n_dp, held_rows, 128), f32),
            partial,
            pltpu.VMEM((8, 128), f32),
            pltpu.VMEM((n_seq, 8, 128), f32),
            pltpu.VMEM((8, 128), f32),
            pltpu.VMEM((n_dp, 8, 128), f32),
            pltpu.SemaphoreType.DMA((6,)),
            utt_sems,
            utt_sems,
            utt_sems,
            utt_sems,
            pltpu.SemaphoreType.DMA((4 * utts,)),
            pltpu.SemaphoreType.DMA((4 * utts,)),
            seq_sems,
            seq_sems,
            dp_sems,
            dp_sems,
            seq_sems,
            seq_sems,
            seq_sems,
            seq_sems,
            dp_sems,
            dp_sems,
        ],
        compiler_params=pltpu.CompilerParams(
            collective_id=2, has_side_effects=True, vmem_limit_bytes=56 * 2**20
        ),
    )(
        utt_lengths,
        picks,
        conv_kernel,
        queries,
        key_rows,
        value_rows,
        layer_input,
        conv_cotangent,
        out_weight,
    )
    flat_total = total.reshape(-1)
    weight_picks = flat_total[: pick_weight.shape[0]]
    kernel_picks = tile.reshape(-1)[: pick_kernel.shape[0]]
    return (conv_out, context_grad, weight_picks, kernel_picks)


def on_device(
    queries,
    key_rows,
    value_rows,
    layer_input,
    utt_lengths,
    out_weight,
    conv_kernel,
    conv_cotangent,
    pick_weight,
    pick_kernel,
):
    local_utts, frames_dev, width = queries.shape
    seq_count = lax.axis_size("seq")
    if HEADS % seq_count == 0:
        return one_kernel(
            queries,
            key_rows,
            value_rows,
            layer_input,
            utt_lengths,
            out_weight,
            conv_kernel,
            conv_cotangent,
            pick_weight,
            pick_kernel,
        )
    full_frames = frames_dev * seq_count
    head_size = width // HEADS
    score_scale = 1.0 / math.sqrt(head_size)
    first_frame = lax.axis_index("seq") * frames_dev
    local_ids = first_frame + jnp.arange(frames_dev, dtype=jnp.int32)
    valid_rows = (local_ids[None, :] < utt_lengths[:, None]).astype(jnp.float32)
    context = gathered_attention(queries, key_rows, value_rows, utt_lengths, score_scale)
    context_flat = context.reshape(local_utts * frames_dev, width)
    projected = jnp.dot(context_flat, out_weight, preferred_element_type=jnp.float32).reshape(
        local_utts, frames_dev, width
    )
    hidden = ((layer_input.astype(jnp.float32) + projected) * valid_rows[:, :, None]).astype(
        jnp.bfloat16
    )
    tap_count = conv_kernel.shape[0]
    half_taps = (tap_count - 1) // 2
    kernel_f = conv_kernel.astype(jnp.float32)
    hidden_pad = padded(hidden, (("seq", 1),), half_taps)
    cot_f = conv_cotangent.astype(jnp.float32)
    conv_sum = jnp.zeros((local_utts, frames_dev, width), jnp.float32)
    kernel_rows = []
    for offset in range(tap_count):
        window = hidden_pad[:, offset : offset + frames_dev].astype(jnp.float32)
        conv_sum = conv_sum + kernel_f[offset] * window
        kernel_rows.append(jnp.sum(window * cot_f, axis=(0, 1)))
    conv_out = conv_sum.astype(jnp.bfloat16)
    kernel_grad = jnp.stack(kernel_rows)
    cot_pad = padded(conv_cotangent, (("seq", 1),), half_taps).astype(jnp.float32)
    back_sum = jnp.zeros((local_utts, frames_dev, width), jnp.float32)
    for offset in range(tap_count):
        begin = 2 * half_taps - offset
        back_sum = back_sum + kernel_f[offset] * cot_pad[:, begin : begin + frames_dev]
    hidden_grad = (back_sum * valid_rows[:, :, None]).astype(jnp.bfloat16)
    grad_flat = hidden_grad.reshape(local_utts * frames_dev, width)
    context_grad = lax.dot_general(
        grad_flat, out_weight, (((1,), (1,)), ((), ())), preferred_element_type=jnp.float32
    )
    context_grad = context_grad.reshape(local_utts, frames_dev, width).astype(jnp.bfloat16)
    weight_vals = picked_products(context_flat, grad_flat, pick_weight)
    kernel_vals = pick_entries(kernel_grad, pick_kernel)
    total = summed(jnp.concatenate([weight_vals, kernel_vals]))
    weight_sum = total[: pick_weight.shape[0]]
    kernel_sum = total[weight_vals.shape[0] : weight_vals.shape[0] + pick_kernel.shape[0]]
    total_slots = local_utts * lax.axis_size("dp") * full_frames
    norm_factor = 1.0 / math.sqrt(total_slots)
    return (conv_out, context_grad, weight_sum * norm_factor, kernel_sum * norm_factor)


def solution(mesh):
    placed = (
        P("dp", "seq", None),
        P("dp", "seq", None),
        P("dp", "seq", None),
        P("dp", "seq", None),
        P("dp"),
        P(),
        P(),
        P("dp", "seq", None),
        P(),
        P(),
    )
    return jax.shard_map(
        on_device,
        mesh=mesh,
        in_specs=placed,
        out_specs=(P("dp", "seq", None), P("dp", "seq", None), P(), P()),
        check_vma=False,
    )
```

```python
import functools
import math

import jax
import jax.numpy as jnp
from jax import lax
from jax.experimental import pallas as pl
from jax.experimental.pallas import tpu as pltpu
from jax.sharding import PartitionSpec as P

HEADS = 16


neg_big = -1e30


def padded(value, sides, width):
    for axis, dim in sides:
        count, length = (lax.axis_size(axis), value.shape[dim])
        up = [(i, (i + 1) % count) for i in range(count - 1)]
        down = [(j, i) for i, j in up]
        last = lax.slice_in_dim(value, length - width, length, axis=dim)
        leading = lax.slice_in_dim(value, 0, width, axis=dim)
        before = lax.ppermute(last, axis, up)
        after = lax.ppermute(leading, axis, down)
        value = jnp.concatenate([before, value, after], axis=dim)
    return value


def softmax_rows(scores, key_ok):
    scores = jnp.where(key_ok, scores, neg_big)
    row_max = jnp.max(scores, axis=-1, keepdims=True)
    probs = jnp.exp(scores - row_max)
    return (probs.astype(jnp.bfloat16), jnp.sum(probs, axis=-1))


def pick_entries(table, picks):
    flat = table.reshape(-1)
    lane = math.gcd(flat.shape[0], 128)
    blocks = flat.reshape(flat.shape[0] // lane, lane)
    chosen = jnp.take(blocks, picks // lane, axis=0)
    lane_ids = jnp.arange(lane, dtype=jnp.int32)
    hit = lane_ids[None, :] == (picks % lane)[:, None]
    return jnp.sum(jnp.where(hit, chosen, jnp.float32(0.0)), axis=1)


def peers_of(axis, count):
    me = lax.axis_index(axis)
    return [lax.rem(me + step, count) for step in range(1, count)]


def greet(axes):
    barrier = pltpu.get_barrier_semaphore()
    total = 0
    for axis, count in axes:
        for peer in peers_of(axis, count):
            pl.semaphore_signal(
                barrier, inc=1, device_id={axis: peer}, device_id_type=pl.DeviceIdType.MESH
            )
            total += 1
    pl.semaphore_wait(barrier, total)


def send_to(src, dst, send_sem, recv_sem, axis, peer):
    copy = pltpu.make_async_remote_copy(
        src_ref=src,
        dst_ref=dst,
        send_sem=send_sem,
        recv_sem=recv_sem,
        device_id={axis: peer},
        device_id_type=pl.DeviceIdType.MESH,
    )
    copy.start()
    return copy


def total_kernel(
    n_seq, n_dp, x_ref, out_ref, parts, mine, sums, whole, s1, r1, s2, r2, s3, r3
):
    me = lax.axis_index("seq")
    me_dp = lax.axis_index("dp")
    greet((("seq", n_seq), ("dp", n_dp)))
    copies = [
        send_to(x_ref.at[peer], parts.at[me], s1.at[i], r1.at[i], "seq", peer)
        for i, peer in enumerate(peers_of("seq", n_seq))
    ]
    parts[pl.ds(me, 1)] = x_ref[pl.ds(me, 1)]
    for copy in copies:
        copy.wait_recv()
    mine[...] = jnp.sum(parts[...], axis=0)
    second = [
        send_to(mine, sums.at[me_dp], s2.at[i], r2.at[i], "dp", peer)
        for i, peer in enumerate(peers_of("dp", n_dp))
    ]
    sums[pl.ds(me_dp, 1)] = mine[...][None]
    for copy in second:
        copy.wait_recv()
    whole[pl.ds(me, 1)] = jnp.sum(sums[...], axis=0)[None]
    third = [
        send_to(whole.at[me], whole.at[me], s3.at[i], r3.at[i], "seq", peer)
        for i, peer in enumerate(peers_of("seq", n_seq))
    ]
    for copy in third:
        copy.wait_recv()
    out_ref[...] = whole[...]
    for copy in copies + second + third:
        copy.wait_send()


def summed(values):
    n_seq, n_dp = lax.axis_size("seq"), lax.axis_size("dp")
    chunk = 128 * 8 * n_seq
    rows = -(-values.shape[0] // chunk) * 8
    x = jnp.pad(values, (0, rows * 128 * n_seq - values.shape[0])).reshape(n_seq, rows, 128)
    vmem = pl.BlockSpec(memory_space=pltpu.VMEM)
    seq_sems = pltpu.SemaphoreType.DMA((n_seq - 1,))
    dp_sems = pltpu.SemaphoreType.DMA((n_dp - 1,))
    out = pl.pallas_call(
        functools.partial(total_kernel, n_seq, n_dp),
        out_shape=jax.ShapeDtypeStruct(x.shape, jnp.float32),
        in_specs=[vmem],
        out_specs=vmem,
        scratch_shapes=[
            pltpu.VMEM(x.shape, jnp.float32),
            pltpu.VMEM((rows, 128), jnp.float32),
            pltpu.VMEM((n_dp, rows, 128), jnp.float32),
            pltpu.VMEM(x.shape, jnp.float32),
            seq_sems,
            seq_sems,
            dp_sems,
            dp_sems,
            seq_sems,
            seq_sems,
        ],
        compiler_params=pltpu.CompilerParams(collective_id=1, has_side_effects=True),
    )(x)
    return out.reshape(-1)


LOW = 256
PICK_TILE = 512


def choose(stacked, tokens, index):
    low = lax.rem(index, LOW)
    high = lax.div(index, LOW)
    ids = lax.broadcasted_iota(jnp.int32, (LOW, index.shape[1]), 0).astype(jnp.bfloat16)
    one, zero = jnp.bfloat16(1.0), jnp.bfloat16(0.0)
    hot = jnp.where(ids == low.astype(jnp.bfloat16), one, zero)
    every = jnp.dot(stacked, hot, preferred_element_type=jnp.float32)
    out = every[:tokens]
    for part in range(1, stacked.shape[0] // tokens):
        out = jnp.where(high == part, every[part * tokens : (part + 1) * tokens], out)
    return out


GROUP = 16


def one_hot(low):
    ids = lax.broadcasted_iota(jnp.int32, (LOW, low.shape[1]), 0).astype(jnp.bfloat16)
    one, zero = jnp.bfloat16(1.0), jnp.bfloat16(0.0)
    return jnp.where(ids == low.astype(jnp.bfloat16), one, zero)


def choose_groups(stacked, tokens, index):
    parts = stacked.shape[0] // tokens
    high = lax.div(index, LOW)
    every = jnp.dot(
        stacked, one_hot(lax.rem(index, LOW)), preferred_element_type=jnp.float32
    )
    for group in range(tokens // GROUP):
        begin = group * parts * GROUP
        out = every[begin : begin + GROUP]
        for part in range(1, parts):
            place = begin + part * GROUP
            out = jnp.where(high == part, every[place : place + GROUP], out)
        yield group * GROUP, out


def stack_groups(stack, rows, first_row, parts):
    for group in range(rows.shape[0] // GROUP):
        for part in range(parts):
            begin = (first_row // GROUP + group) * parts * GROUP + part * GROUP
            stack[begin : begin + GROUP, :] = rows[
                group * GROUP : (group + 1) * GROUP, part * LOW : (part + 1) * LOW
            ]


def picks_kernel(pick_ref, ctx_ref, grad_ref, out_ref, ctx_stack, grad_stack):
    tokens, width = ctx_ref.shape

    @pl.when(pl.program_id(0) == 0)
    def _():
        for part in range(width // LOW):
            cols = slice(part * LOW, (part + 1) * LOW)
            rows = slice(part * tokens, (part + 1) * tokens)
            ctx_stack[rows, :] = ctx_ref[:, cols]
            grad_stack[rows, :] = grad_ref[:, cols]

    pick = pick_ref[...]
    left = choose(ctx_stack[...], tokens, lax.div(pick, width))
    right = choose(grad_stack[...], tokens, lax.rem(pick, width))
    out_ref[...] = jnp.sum(left * right, axis=0, keepdims=True)


def picked_products(ctx, grad, picks):
    tokens, width = ctx.shape
    steps = -(-picks.shape[0] // PICK_TILE)
    padded_picks = jnp.pad(picks, (0, steps * PICK_TILE - picks.shape[0])).reshape(1, -1)
    whole = pl.BlockSpec((tokens, width), lambda i: (0, 0))
    tile = pl.BlockSpec((1, PICK_TILE), lambda i: (0, i))
    stack = pltpu.VMEM((tokens * width // LOW, LOW), jnp.bfloat16)
    out = pl.pallas_call(
        picks_kernel,
        grid=(steps,),
        out_shape=jax.ShapeDtypeStruct(padded_picks.shape, jnp.float32),
        in_specs=[tile, whole, whole],
        out_specs=tile,
        scratch_shapes=[stack, stack],
        compiler_params=pltpu.CompilerParams(vmem_limit_bytes=40 * 2**20),
    )(padded_picks, ctx, grad)
    return out.reshape(-1)


def gathered_attention(queries, key_rows, value_rows, utt_lengths, score_scale):
    local_utts, frames_dev, width = queries.shape
    full_frames = frames_dev * lax.axis_size("seq")
    head_size = width // HEADS
    all_keys, all_values = (
        lax.all_gather(key_rows, "seq", axis=1, tiled=True),
        lax.all_gather(value_rows, "seq", axis=1, tiled=True),
    )
    full_ids = jnp.arange(full_frames, dtype=jnp.int32)

    def one_utt(item):
        query_utt, key_utt, value_utt, length_utt = item
        query_heads = query_utt.reshape(frames_dev, HEADS, head_size)
        key_heads = key_utt.reshape(full_frames, HEADS, head_size)
        value_heads = value_utt.reshape(full_frames, HEADS, head_size)
        scores = (
            jnp.einsum("qhd,khd->hqk", query_heads, key_heads, preferred_element_type=jnp.float32)
            * score_scale
        )
        weights, denom = softmax_rows(scores, (full_ids < length_utt)[None, None, :])
        out_rows = jnp.einsum(
            "hqk,khd->qhd", weights, value_heads, preferred_element_type=jnp.float32
        )
        out_rows = out_rows / denom.transpose(1, 0)[:, :, None]
        return out_rows.astype(jnp.bfloat16).reshape(frames_dev, width)

    return lax.map(one_utt, (queries, all_keys, all_values, utt_lengths))


def shifted_windows(chunk, frames):
    for turn in range(8):
        part = chunk[turn : turn + frames + 24]
        for eight in range(4):
            offset = 8 * eight + turn
            if 1 <= offset <= 31:
                yield offset, part[8 * eight : 8 * eight + frames]


def block_kernel(
    n_seq,
    n_dp,
    rows_each,
    score_scale,
    norm_factor,
    len_ref,
    pick_ref,
    kern_ref,
    q_hbm,
    k_hbm,
    v_hbm,
    in_hbm,
    cot_hbm,
    w_hbm,
    conv_ref,
    cgrad_ref,
    sum_ref,
    tile_ref,
    q_ref,
    k_ref,
    v_ref,
    in_ref,
    cot_ref,
    w_ref,
    send,
    recv,
    back,
    home,
    cot_edge,
    hid_edge,
    cot_pad,
    hid_pad,
    hidden,
    grad,
    grad_stack,
    ctx,
    ctx_stack,
    grad_picked,
    kern_grad,
    x_ref,
    parts,
    mine,
    sums,
    whole,
    tile,
    tile_parts,
    tile_mine,
    tile_sums,
    load_sem,
    send_sem,
    recv_sem,
    back_sem,
    home_sem,
    edge_send,
    edge_recv,
    s1,
    r1,
    s2,
    r2,
    s3,
    r3,
    s4,
    r4,
    s5,
    r5,
):
    utts, frames, width = q_ref.shape
    taps = kern_ref.shape[0]
    lanes = PICK_TILE // 128
    held = rows_each * lanes
    reach = 16
    tokens = utts * frames
    block = width // n_seq
    head_size = width // HEADS
    me = lax.axis_index("seq")
    me_dp = lax.axis_index("dp")
    right, left = lax.rem(me + 1, n_seq), lax.rem(me + n_seq - 1, n_seq)
    loads = [
        pltpu.make_async_copy(src, dst, load_sem.at[i])
        for i, (src, dst) in enumerate(
            (
                (cot_hbm, cot_ref),
                (q_hbm, q_ref),
                (k_hbm, k_ref),
                (v_hbm, v_ref),
                (w_hbm, w_ref),
                (in_hbm, in_ref),
            )
        )
    ]
    for load in loads:
        load.start()
    greet((("seq", n_seq), ("dp", n_dp)))

    def swap_edges(rows, edge, utt, base):
        return [
            send_to(
                rows.at[utt, frames - reach : frames],
                edge.at[0, utt],
                edge_send.at[base],
                edge_recv.at[base],
                "seq",
                right,
            ),
            send_to(
                rows.at[utt, 0:reach],
                edge.at[1, utt],
                edge_send.at[base + 1],
                edge_recv.at[base + 1],
                "seq",
                left,
            ),
        ]

    def pad_edges(edge, pad):
        for utt in range(utts):
            before = edge[0, utt].astype(jnp.float32)
            after = edge[1, utt].astype(jnp.float32)
            pad[utt, 0:reach, :] = jnp.where(me > 0, before, 0.0)
            pad[utt, reach + frames : 2 * reach + frames, :] = jnp.where(
                me < n_seq - 1, after, 0.0
            )

    half = frames // 2

    def send_heads(utt):
        for owner in range(n_seq):
            for part in range(2):
                for place, ref in enumerate((q_ref, k_ref, v_ref)):
                    begin = (part * 3 + place) * block
                    send[utt, owner, :, begin : begin + block] = ref[
                        utt, part * half : (part + 1) * half, owner * block : (owner + 1) * block
                    ]
        sent = [
            send_to(
                send.at[utt, peer],
                recv.at[utt, me],
                send_sem.at[utt, i],
                recv_sem.at[utt, i],
                "seq",
                peer,
            )
            for i, peer in enumerate(peers_of("seq", n_seq))
        ]
        recv[utt, pl.ds(me, 1)] = send[utt, pl.ds(me, 1)]
        return sent

    def attend(utt):
        full = n_seq * frames
        key_ok = lax.broadcasted_iota(jnp.int32, (full, full), 1) < len_ref[utt]
        for head in range(block // head_size):
            three = []
            for place in range(3):
                pieces = []
                for part in range(2):
                    begin = (part * 3 + place) * block + head * head_size
                    pieces.append(recv[utt, :, :, begin : begin + head_size])
                three.append(jnp.concatenate(pieces, axis=1).reshape(full, head_size))
            query, key, value = three
            scores = lax.dot_general(
                query, key, (((1,), (1,)), ((), ())), preferred_element_type=jnp.float32
            )
            scores = jnp.where(key_ok, scores * score_scale, neg_big)
            probs = jnp.exp(scores - jnp.max(scores, axis=-1, keepdims=True))
            denom = jnp.sum(probs, axis=-1, keepdims=True)
            rows = jnp.dot(probs.astype(jnp.bfloat16), value, preferred_element_type=jnp.float32)
            rows = (rows / denom).astype(jnp.bfloat16).reshape(n_seq, frames, head_size)
            for part in range(2):
                begin = part * block + head * head_size
                back[utt, :, :, begin : begin + head_size] = rows[
                    :, part * half : (part + 1) * half
                ]
        sent = [
            send_to(
                back.at[utt, peer],
                home.at[utt, me],
                back_sem.at[utt, i],
                home_sem.at[utt, i],
                "seq",
                peer,
            )
            for i, peer in enumerate(peers_of("seq", n_seq))
        ]
        home[utt, pl.ds(me, 1)] = back[utt, pl.ds(me, 1)]
        return sent

    def project(utt):
        first_row = utt * frames
        for owner in range(n_seq):
            for part in range(2):
                rows = slice(first_row + part * half, first_row + (part + 1) * half)
                ctx[rows, owner * block : (owner + 1) * block] = home[
                    utt, owner, :, part * block : (part + 1) * block
                ]
        rows = slice(first_row, first_row + frames)

        @pl.loop(0, width // LOW)
        def _(step):
            cols = pl.ds(pl.multiple_of(step * LOW, LOW), LOW)
            value = jnp.dot(ctx[rows, :], w_ref[:, cols], preferred_element_type=jnp.float32)
            value = in_ref[utt, :, cols].astype(jnp.float32) + value
            value = jnp.where(frame_ids < len_ref[utt], value, 0.0).astype(jnp.bfloat16)
            hidden[utt, :, cols] = value
            hid_pad[utt, reach : reach + frames, cols] = value.astype(jnp.float32)

        sent = swap_edges(hidden, hid_edge, utt, 2 * utts + 2 * utt)
        stack_groups(ctx_stack, ctx[rows, :], first_row, width // LOW)
        return sent

    def pick_context():
        @pl.loop(0, n_seq)
        def _(owner):
            for row in range(rows_each):
                index = lax.div(pick_row(owner, row), width)
                total = jnp.zeros((GROUP, PICK_TILE), jnp.float32)
                for begin, found in choose_groups(ctx_stack[...], tokens, index):
                    other = grad_picked[owner, row, begin : begin + GROUP, :]
                    total = total + found * other.astype(jnp.float32)
                store_row(x_ref.at[owner], row, jnp.sum(total, axis=0, keepdims=True))

    def pick_row(owner, row):
        return jnp.concatenate(
            [pick_ref[owner, lanes * row + i : lanes * row + i + 1, :] for i in range(lanes)],
            axis=1,
        )

    def store_row(ref, row, value):
        for i in range(lanes):
            place = slice(lanes * row + i, lanes * row + i + 1)
            ref[place, :] = value[:, i * 128 : (i + 1) * 128]

    for load in loads[:4]:
        load.wait()
    copies = send_heads(0)
    edges = []
    for utt in range(utts):
        edges += swap_edges(cot_ref, cot_edge, utt, 2 * utt)

    frame_ids = me * frames + lax.broadcasted_iota(jnp.int32, (frames, 1), 0)
    for utt in range(utts):
        cot_pad[utt, reach : reach + frames, :] = cot_ref[utt].astype(jnp.float32)
    for copy in edges:
        copy.wait_recv()
    pad_edges(cot_edge, cot_pad)

    @pl.loop(0, width // 128)
    def _(step):
        cols = pl.ds(pl.multiple_of(step * 128, 128), 128)
        kern = kern_ref[:, cols].astype(jnp.float32)
        for utt in range(utts):
            total = jnp.zeros((frames, 128), jnp.float32)
            for offset, window in shifted_windows(cot_pad[utt, :, cols], frames):
                tap = taps - offset
                total = total + kern[tap : tap + 1] * window
            total = jnp.where(frame_ids < len_ref[utt], total, 0.0)
            grad[utt * frames : (utt + 1) * frames, cols] = total.astype(jnp.bfloat16)

    stack_groups(grad_stack, grad[...], 0, width // LOW)

    def pick_grad(begin, end):
        @pl.loop(begin, end)
        def _(owner):
            for row in range(rows_each):
                index = lax.rem(pick_row(owner, row), width)
                for begin, found in choose_groups(grad_stack[...], tokens, index):
                    grad_picked[owner, row, begin : begin + GROUP, :] = found.astype(jnp.bfloat16)

    for utt in range(1, utts):
        copies += send_heads(utt)
    pick_grad(0, n_seq)
    returns = []
    for utt in range(utts):
        for copy in copies[utt * (n_seq - 1) : (utt + 1) * (n_seq - 1)]:
            copy.wait_recv()
        returns += attend(utt)
    loads[4].wait()
    loads[5].wait()

    @pl.loop(0, width // LOW)
    def _(step):
        cols = pl.ds(pl.multiple_of(step * LOW, LOW), LOW)
        value = lax.dot_general(
            grad[...], w_ref[cols, :], (((1,), (1,)), ((), ())), preferred_element_type=jnp.float32
        ).astype(jnp.bfloat16)
        for row in range(utts):
            cgrad_ref[row, :, cols] = value[row * frames : (row + 1) * frames]

    hid_copies = []
    for utt in range(utts):
        for copy in returns[utt * (n_seq - 1) : (utt + 1) * (n_seq - 1)]:
            copy.wait_recv()
        hid_copies += project(utt)
    pick_context()
    first = [
        send_to(x_ref.at[peer], parts.at[me], s1.at[i], r1.at[i], "seq", peer)
        for i, peer in enumerate(peers_of("seq", n_seq))
    ]
    parts[pl.ds(me, 1)] = x_ref[pl.ds(me, 1)]
    for copy in hid_copies:
        copy.wait_recv()
    pad_edges(hid_edge, hid_pad)
    kern_grad[...] = jnp.zeros_like(kern_grad)

    @pl.loop(0, width // 128)
    def _(step):
        cols = pl.ds(pl.multiple_of(step * 128, 128), 128)
        found = {}
        for utt in range(utts):
            cot = cot_pad[utt, reach : reach + frames, cols]
            for offset, window in shifted_windows(hid_pad[utt, :, cols], frames):
                value = jnp.sum((window * cot).reshape(frames // 8, 8, 128), axis=0)
                found[offset] = value if utt == 0 else found[offset] + value
        for offset, value in found.items():
            kern_grad[offset - 1 : offset, cols] = jnp.sum(value, axis=0, keepdims=True)

    pick = pick_row(n_seq - 1, rows_each - 1)
    rest = jnp.concatenate(
        [kern_grad[:, part * LOW : (part + 1) * LOW] for part in range(width // LOW)], axis=0
    )
    found = jnp.zeros((kern_grad.shape[0], PICK_TILE), jnp.float32)
    for _ in range(3):
        piece = rest.astype(jnp.bfloat16)
        rest = rest - piece.astype(jnp.float32)
        found = found + choose(piece, kern_grad.shape[0], lax.rem(pick, width))
    tap_ids = lax.broadcasted_iota(jnp.int32, found.shape, 0)
    found = jnp.where(tap_ids == lax.div(pick, width), found, 0.0)
    tile[...] = jnp.zeros_like(tile)
    store_row(tile, 0, jnp.sum(found, axis=0, keepdims=True))

    tile_first = [
        send_to(tile, tile_parts.at[me], s4.at[i], r4.at[i], "seq", peer)
        for i, peer in enumerate(peers_of("seq", n_seq))
    ]
    tile_parts[pl.ds(me, 1)] = tile[...][None]

    def convolve(begin, end):
        @pl.loop(begin, end)
        def _(step):
            cols = pl.ds(pl.multiple_of(step * 128, 128), 128)
            kern = kern_ref[:, cols].astype(jnp.float32)
            for utt in range(utts):
                total = jnp.zeros((frames, 128), jnp.float32)
                for offset, window in shifted_windows(hid_pad[utt, :, cols], frames):
                    total = total + kern[offset - 1 : offset] * window
                conv_ref[utt, :, cols] = total.astype(jnp.bfloat16)

    third_part = width // 128 // 3
    for copy in first:
        copy.wait_recv()
    mine[...] = jnp.sum(parts[...], axis=0)
    second = [
        send_to(mine, sums.at[me_dp], s2.at[i], r2.at[i], "dp", peer)
        for i, peer in enumerate(peers_of("dp", n_dp))
    ]
    sums[pl.ds(me_dp, 1)] = mine[...][None]
    convolve(0, third_part)
    for copy in tile_first:
        copy.wait_recv()
    tile_mine[...] = jnp.sum(tile_parts[...], axis=0)
    tile_second = [
        send_to(tile_mine, tile_sums.at[me_dp], s5.at[i], r5.at[i], "dp", peer)
        for i, peer in enumerate(peers_of("dp", n_dp))
    ]
    tile_sums[pl.ds(me_dp, 1)] = tile_mine[...][None]
    for copy in second:
        copy.wait_recv()
    whole[pl.ds(me, 1)] = (jnp.sum(sums[...], axis=0) * norm_factor)[None]
    third = [
        send_to(whole.at[me], whole.at[me], s3.at[i], r3.at[i], "seq", peer)
        for i, peer in enumerate(peers_of("seq", n_seq))
    ]
    convolve(third_part, width // 128)
    for copy in tile_second:
        copy.wait_recv()
    tile_ref[...] = jnp.sum(tile_sums[...], axis=0)[: tile_ref.shape[0]] * norm_factor
    for copy in third:
        copy.wait_recv()
    for owner in range(n_seq):
        sum_ref[owner * held : (owner + 1) * held] = whole[owner]
    for copy in edges + copies + returns + hid_copies + first + second + third:
        copy.wait_send()
    for copy in tile_first + tile_second:
        copy.wait_send()


def write_kernel(count, *refs):
    sources, outs, held = refs[:count], refs[count : 2 * count], refs[2 * count : 3 * count]
    in_sems, out_sems = refs[3 * count :]
    reads = [pltpu.make_async_copy(sources[i], held[i], in_sems.at[i]) for i in range(count)]
    writes = [pltpu.make_async_copy(held[i], outs[i], out_sems.at[i]) for i in range(count)]
    for copy in reads:
        copy.start()
    for read, write in zip(reads, writes):
        read.wait()
        write.start()
    for copy in writes:
        copy.wait()


def written(*arrays):
    spec = pl.BlockSpec(memory_space=pl.ANY)
    count = len(arrays)
    sems = pltpu.SemaphoreType.DMA((count,))
    return pl.pallas_call(
        functools.partial(write_kernel, count),
        out_shape=[jax.ShapeDtypeStruct(array.shape, array.dtype) for array in arrays],
        in_specs=[spec] * count,
        out_specs=[spec] * count,
        scratch_shapes=[pltpu.VMEM(array.shape, array.dtype) for array in arrays] + [sems, sems],
        compiler_params=pltpu.CompilerParams(vmem_limit_bytes=56 * 2**20),
    )(*arrays)


def one_kernel(
    queries,
    key_rows,
    value_rows,
    layer_input,
    utt_lengths,
    out_weight,
    conv_kernel,
    conv_cotangent,
    pick_weight,
    pick_kernel,
):
    utts, frames, width = queries.shape
    n_seq, n_dp = lax.axis_size("seq"), lax.axis_size("dp")
    block = width // n_seq
    tokens = utts * frames
    tiles = -(-pick_weight.shape[0] // PICK_TILE) + 1
    rows_each = -(-tiles // (2 * n_seq)) * 2
    held_rows = rows_each * PICK_TILE // 128
    kernel_start = (rows_each * n_seq - 1) * PICK_TILE
    picks = jnp.concatenate(
        [
            jnp.pad(pick_weight, (0, kernel_start - pick_weight.shape[0])),
            jnp.pad(pick_kernel, (0, PICK_TILE - pick_kernel.shape[0])),
        ]
    ).reshape(n_seq, held_rows, 128)
    vmem = pl.BlockSpec(memory_space=pltpu.VMEM)
    hbm = pl.BlockSpec(memory_space=pl.ANY)
    bf16, f32 = jnp.bfloat16, jnp.float32
    local = pltpu.VMEM((utts, frames, width), bf16)
    wide = pltpu.VMEM((utts, n_seq, frames // 2, 6 * block), bf16)
    narrow = pltpu.VMEM((utts, n_seq, frames // 2, 2 * block), bf16)
    edge = pltpu.VMEM((2, utts, 16, width), bf16)
    pad = pltpu.VMEM((utts, frames + 32, width), f32)
    flat = pltpu.VMEM((tokens, width), bf16)
    stack = pltpu.VMEM((tokens * width // LOW, LOW), bf16)
    partial = pltpu.VMEM((n_seq, held_rows, 128), f32)
    seq_sems = pltpu.SemaphoreType.DMA((n_seq - 1,))
    dp_sems = pltpu.SemaphoreType.DMA((n_dp - 1,))
    utt_sems = pltpu.SemaphoreType.DMA((utts, n_seq - 1))
    score_scale = 1.0 / math.sqrt(width // HEADS)
    norm_factor = 1.0 / math.sqrt(utts * n_dp * frames * n_seq)
    conv_out, context_grad, total, tile = pl.pallas_call(
        functools.partial(block_kernel, n_seq, n_dp, rows_each, score_scale, norm_factor),
        out_shape=(
            jax.ShapeDtypeStruct(queries.shape, bf16),
            jax.ShapeDtypeStruct(queries.shape, bf16),
            jax.ShapeDtypeStruct((n_seq * held_rows, 128), f32),
            jax.ShapeDtypeStruct((PICK_TILE // 128, 128), f32),
        ),
        in_specs=[pl.BlockSpec(memory_space=pltpu.SMEM), vmem, vmem] + [hbm] * 6,
        out_specs=(vmem, vmem, vmem, vmem),
        scratch_shapes=[
            local,
            local,
            local,
            local,
            local,
            pltpu.VMEM((width, width), bf16),
            wide,
            wide,
            narrow,
            narrow,
            edge,
            edge,
            pad,
            pad,
            local,
            flat,
            stack,
            flat,
            stack,
            pltpu.VMEM((n_seq, rows_each, tokens, PICK_TILE), bf16),
            pltpu.VMEM((32, width), f32),
            partial,
            partial,
            pltpu.VMEM((held_rows, 128), f32),
            pltpu.VMEM((n_dp, held_rows, 128), f32),
            partial,
            pltpu.VMEM((8, 128), f32),
            pltpu.VMEM((n_seq, 8, 128), f32),
            pltpu.VMEM((8, 128), f32),
            pltpu.VMEM((n_dp, 8, 128), f32),
            pltpu.SemaphoreType.DMA((6,)),
            utt_sems,
            utt_sems,
            utt_sems,
            utt_sems,
            pltpu.SemaphoreType.DMA((4 * utts,)),
            pltpu.SemaphoreType.DMA((4 * utts,)),
            seq_sems,
            seq_sems,
            dp_sems,
            dp_sems,
            seq_sems,
            seq_sems,
            seq_sems,
            seq_sems,
            dp_sems,
            dp_sems,
        ],
        compiler_params=pltpu.CompilerParams(
            collective_id=2, has_side_effects=True, vmem_limit_bytes=56 * 2**20
        ),
    )(
        utt_lengths,
        picks,
        conv_kernel,
        queries,
        key_rows,
        value_rows,
        layer_input,
        conv_cotangent,
        out_weight,
    )
    conv_out, context_grad, total, tile = written(conv_out, context_grad, total, tile)
    flat_total = total.reshape(-1)
    weight_picks = flat_total[: pick_weight.shape[0]]
    kernel_picks = tile.reshape(-1)[: pick_kernel.shape[0]]
    return (conv_out, context_grad, weight_picks, kernel_picks)


def on_device(
    queries,
    key_rows,
    value_rows,
    layer_input,
    utt_lengths,
    out_weight,
    conv_kernel,
    conv_cotangent,
    pick_weight,
    pick_kernel,
):
    local_utts, frames_dev, width = queries.shape
    seq_count = lax.axis_size("seq")
    if HEADS % seq_count == 0:
        return one_kernel(
            queries,
            key_rows,
            value_rows,
            layer_input,
            utt_lengths,
            out_weight,
            conv_kernel,
            conv_cotangent,
            pick_weight,
            pick_kernel,
        )
    full_frames = frames_dev * seq_count
    head_size = width // HEADS
    score_scale = 1.0 / math.sqrt(head_size)
    first_frame = lax.axis_index("seq") * frames_dev
    local_ids = first_frame + jnp.arange(frames_dev, dtype=jnp.int32)
    valid_rows = (local_ids[None, :] < utt_lengths[:, None]).astype(jnp.float32)
    context = gathered_attention(queries, key_rows, value_rows, utt_lengths, score_scale)
    context_flat = context.reshape(local_utts * frames_dev, width)
    projected = jnp.dot(context_flat, out_weight, preferred_element_type=jnp.float32).reshape(
        local_utts, frames_dev, width
    )
    hidden = ((layer_input.astype(jnp.float32) + projected) * valid_rows[:, :, None]).astype(
        jnp.bfloat16
    )
    tap_count = conv_kernel.shape[0]
    half_taps = (tap_count - 1) // 2
    kernel_f = conv_kernel.astype(jnp.float32)
    hidden_pad = padded(hidden, (("seq", 1),), half_taps)
    cot_f = conv_cotangent.astype(jnp.float32)
    conv_sum = jnp.zeros((local_utts, frames_dev, width), jnp.float32)
    kernel_rows = []
    for offset in range(tap_count):
        window = hidden_pad[:, offset : offset + frames_dev].astype(jnp.float32)
        conv_sum = conv_sum + kernel_f[offset] * window
        kernel_rows.append(jnp.sum(window * cot_f, axis=(0, 1)))
    conv_out = conv_sum.astype(jnp.bfloat16)
    kernel_grad = jnp.stack(kernel_rows)
    cot_pad = padded(conv_cotangent, (("seq", 1),), half_taps).astype(jnp.float32)
    back_sum = jnp.zeros((local_utts, frames_dev, width), jnp.float32)
    for offset in range(tap_count):
        begin = 2 * half_taps - offset
        back_sum = back_sum + kernel_f[offset] * cot_pad[:, begin : begin + frames_dev]
    hidden_grad = (back_sum * valid_rows[:, :, None]).astype(jnp.bfloat16)
    grad_flat = hidden_grad.reshape(local_utts * frames_dev, width)
    context_grad = lax.dot_general(
        grad_flat, out_weight, (((1,), (1,)), ((), ())), preferred_element_type=jnp.float32
    )
    context_grad = context_grad.reshape(local_utts, frames_dev, width).astype(jnp.bfloat16)
    weight_vals = picked_products(context_flat, grad_flat, pick_weight)
    kernel_vals = pick_entries(kernel_grad, pick_kernel)
    total = summed(jnp.concatenate([weight_vals, kernel_vals]))
    weight_sum = total[: pick_weight.shape[0]]
    kernel_sum = total[weight_vals.shape[0] : weight_vals.shape[0] + pick_kernel.shape[0]]
    total_slots = local_utts * lax.axis_size("dp") * full_frames
    norm_factor = 1.0 / math.sqrt(total_slots)
    return (conv_out, context_grad, weight_sum * norm_factor, kernel_sum * norm_factor)


def solution(mesh):
    placed = (
        P("dp", "seq", None),
        P("dp", "seq", None),
        P("dp", "seq", None),
        P("dp", "seq", None),
        P("dp"),
        P(),
        P(),
        P("dp", "seq", None),
        P(),
        P(),
    )
    return jax.shard_map(
        on_device,
        mesh=mesh,
        in_specs=placed,
        out_specs=(P("dp", "seq", None), P("dp", "seq", None), P(), P()),
        check_vma=False,
    )
```

```python
import functools
import math

import jax
import jax.numpy as jnp
from jax import lax
from jax.experimental import pallas as pl
from jax.experimental.pallas import tpu as pltpu
from jax.sharding import PartitionSpec as P

HEADS = 16


neg_big = -1e30


def padded(value, sides, width):
    for axis, dim in sides:
        count, length = (lax.axis_size(axis), value.shape[dim])
        up = [(i, (i + 1) % count) for i in range(count - 1)]
        down = [(j, i) for i, j in up]
        last = lax.slice_in_dim(value, length - width, length, axis=dim)
        leading = lax.slice_in_dim(value, 0, width, axis=dim)
        before = lax.ppermute(last, axis, up)
        after = lax.ppermute(leading, axis, down)
        value = jnp.concatenate([before, value, after], axis=dim)
    return value


def softmax_rows(scores, key_ok):
    scores = jnp.where(key_ok, scores, neg_big)
    row_max = jnp.max(scores, axis=-1, keepdims=True)
    probs = jnp.exp(scores - row_max)
    return (probs.astype(jnp.bfloat16), jnp.sum(probs, axis=-1))


def pick_entries(table, picks):
    flat = table.reshape(-1)
    lane = math.gcd(flat.shape[0], 128)
    blocks = flat.reshape(flat.shape[0] // lane, lane)
    chosen = jnp.take(blocks, picks // lane, axis=0)
    lane_ids = jnp.arange(lane, dtype=jnp.int32)
    hit = lane_ids[None, :] == (picks % lane)[:, None]
    return jnp.sum(jnp.where(hit, chosen, jnp.float32(0.0)), axis=1)


def peers_of(axis, count):
    me = lax.axis_index(axis)
    return [lax.rem(me + step, count) for step in range(1, count)]


def greet(axes):
    barrier = pltpu.get_barrier_semaphore()
    total = 0
    for axis, count in axes:
        for peer in peers_of(axis, count):
            pl.semaphore_signal(
                barrier, inc=1, device_id={axis: peer}, device_id_type=pl.DeviceIdType.MESH
            )
            total += 1
    pl.semaphore_wait(barrier, total)


def send_to(src, dst, send_sem, recv_sem, axis, peer):
    copy = pltpu.make_async_remote_copy(
        src_ref=src,
        dst_ref=dst,
        send_sem=send_sem,
        recv_sem=recv_sem,
        device_id={axis: peer},
        device_id_type=pl.DeviceIdType.MESH,
    )
    copy.start()
    return copy


def total_kernel(
    n_seq, n_dp, x_ref, out_ref, parts, mine, sums, whole, s1, r1, s2, r2, s3, r3
):
    me = lax.axis_index("seq")
    me_dp = lax.axis_index("dp")
    greet((("seq", n_seq), ("dp", n_dp)))
    copies = [
        send_to(x_ref.at[peer], parts.at[me], s1.at[i], r1.at[i], "seq", peer)
        for i, peer in enumerate(peers_of("seq", n_seq))
    ]
    parts[pl.ds(me, 1)] = x_ref[pl.ds(me, 1)]
    for copy in copies:
        copy.wait_recv()
    mine[...] = jnp.sum(parts[...], axis=0)
    second = [
        send_to(mine, sums.at[me_dp], s2.at[i], r2.at[i], "dp", peer)
        for i, peer in enumerate(peers_of("dp", n_dp))
    ]
    sums[pl.ds(me_dp, 1)] = mine[...][None]
    for copy in second:
        copy.wait_recv()
    whole[pl.ds(me, 1)] = jnp.sum(sums[...], axis=0)[None]
    third = [
        send_to(whole.at[me], whole.at[me], s3.at[i], r3.at[i], "seq", peer)
        for i, peer in enumerate(peers_of("seq", n_seq))
    ]
    for copy in third:
        copy.wait_recv()
    out_ref[...] = whole[...]
    for copy in copies + second + third:
        copy.wait_send()


def summed(values):
    n_seq, n_dp = lax.axis_size("seq"), lax.axis_size("dp")
    chunk = 128 * 8 * n_seq
    rows = -(-values.shape[0] // chunk) * 8
    x = jnp.pad(values, (0, rows * 128 * n_seq - values.shape[0])).reshape(n_seq, rows, 128)
    vmem = pl.BlockSpec(memory_space=pltpu.VMEM)
    seq_sems = pltpu.SemaphoreType.DMA((n_seq - 1,))
    dp_sems = pltpu.SemaphoreType.DMA((n_dp - 1,))
    out = pl.pallas_call(
        functools.partial(total_kernel, n_seq, n_dp),
        out_shape=jax.ShapeDtypeStruct(x.shape, jnp.float32),
        in_specs=[vmem],
        out_specs=vmem,
        scratch_shapes=[
            pltpu.VMEM(x.shape, jnp.float32),
            pltpu.VMEM((rows, 128), jnp.float32),
            pltpu.VMEM((n_dp, rows, 128), jnp.float32),
            pltpu.VMEM(x.shape, jnp.float32),
            seq_sems,
            seq_sems,
            dp_sems,
            dp_sems,
            seq_sems,
            seq_sems,
        ],
        compiler_params=pltpu.CompilerParams(collective_id=1, has_side_effects=True),
    )(x)
    return out.reshape(-1)


LOW = 256
PICK_TILE = 512


def choose(stacked, tokens, index):
    low = lax.rem(index, LOW)
    high = lax.div(index, LOW)
    ids = lax.broadcasted_iota(jnp.int32, (LOW, index.shape[1]), 0).astype(jnp.bfloat16)
    one, zero = jnp.bfloat16(1.0), jnp.bfloat16(0.0)
    hot = jnp.where(ids == low.astype(jnp.bfloat16), one, zero)
    every = jnp.dot(stacked, hot, preferred_element_type=jnp.float32)
    out = every[:tokens]
    for part in range(1, stacked.shape[0] // tokens):
        out = jnp.where(high == part, every[part * tokens : (part + 1) * tokens], out)
    return out


GROUP = 16


def one_hot(low):
    ids = lax.broadcasted_iota(jnp.int32, (LOW, low.shape[1]), 0).astype(jnp.bfloat16)
    one, zero = jnp.bfloat16(1.0), jnp.bfloat16(0.0)
    return jnp.where(ids == low.astype(jnp.bfloat16), one, zero)


def choose_groups(stacked, tokens, index):
    parts = stacked.shape[0] // tokens
    high = lax.div(index, LOW)
    every = jnp.dot(
        stacked, one_hot(lax.rem(index, LOW)), preferred_element_type=jnp.float32
    )
    for group in range(tokens // GROUP):
        begin = group * parts * GROUP
        out = every[begin : begin + GROUP]
        for part in range(1, parts):
            place = begin + part * GROUP
            out = jnp.where(high == part, every[place : place + GROUP], out)
        yield group * GROUP, out


def stack_groups(stack, rows, first_row, parts):
    for group in range(rows.shape[0] // GROUP):
        for part in range(parts):
            begin = (first_row // GROUP + group) * parts * GROUP + part * GROUP
            stack[begin : begin + GROUP, :] = rows[
                group * GROUP : (group + 1) * GROUP, part * LOW : (part + 1) * LOW
            ]


def picks_kernel(pick_ref, ctx_ref, grad_ref, out_ref, ctx_stack, grad_stack):
    tokens, width = ctx_ref.shape

    @pl.when(pl.program_id(0) == 0)
    def _():
        for part in range(width // LOW):
            cols = slice(part * LOW, (part + 1) * LOW)
            rows = slice(part * tokens, (part + 1) * tokens)
            ctx_stack[rows, :] = ctx_ref[:, cols]
            grad_stack[rows, :] = grad_ref[:, cols]

    pick = pick_ref[...]
    left = choose(ctx_stack[...], tokens, lax.div(pick, width))
    right = choose(grad_stack[...], tokens, lax.rem(pick, width))
    out_ref[...] = jnp.sum(left * right, axis=0, keepdims=True)


def picked_products(ctx, grad, picks):
    tokens, width = ctx.shape
    steps = -(-picks.shape[0] // PICK_TILE)
    padded_picks = jnp.pad(picks, (0, steps * PICK_TILE - picks.shape[0])).reshape(1, -1)
    whole = pl.BlockSpec((tokens, width), lambda i: (0, 0))
    tile = pl.BlockSpec((1, PICK_TILE), lambda i: (0, i))
    stack = pltpu.VMEM((tokens * width // LOW, LOW), jnp.bfloat16)
    out = pl.pallas_call(
        picks_kernel,
        grid=(steps,),
        out_shape=jax.ShapeDtypeStruct(padded_picks.shape, jnp.float32),
        in_specs=[tile, whole, whole],
        out_specs=tile,
        scratch_shapes=[stack, stack],
        compiler_params=pltpu.CompilerParams(vmem_limit_bytes=40 * 2**20),
    )(padded_picks, ctx, grad)
    return out.reshape(-1)


def gathered_attention(queries, key_rows, value_rows, utt_lengths, score_scale):
    local_utts, frames_dev, width = queries.shape
    full_frames = frames_dev * lax.axis_size("seq")
    head_size = width // HEADS
    all_keys, all_values = (
        lax.all_gather(key_rows, "seq", axis=1, tiled=True),
        lax.all_gather(value_rows, "seq", axis=1, tiled=True),
    )
    full_ids = jnp.arange(full_frames, dtype=jnp.int32)

    def one_utt(item):
        query_utt, key_utt, value_utt, length_utt = item
        query_heads = query_utt.reshape(frames_dev, HEADS, head_size)
        key_heads = key_utt.reshape(full_frames, HEADS, head_size)
        value_heads = value_utt.reshape(full_frames, HEADS, head_size)
        scores = (
            jnp.einsum("qhd,khd->hqk", query_heads, key_heads, preferred_element_type=jnp.float32)
            * score_scale
        )
        weights, denom = softmax_rows(scores, (full_ids < length_utt)[None, None, :])
        out_rows = jnp.einsum(
            "hqk,khd->qhd", weights, value_heads, preferred_element_type=jnp.float32
        )
        out_rows = out_rows / denom.transpose(1, 0)[:, :, None]
        return out_rows.astype(jnp.bfloat16).reshape(frames_dev, width)

    return lax.map(one_utt, (queries, all_keys, all_values, utt_lengths))


def shifted_windows(chunk, frames):
    for turn in range(8):
        part = chunk[turn : turn + frames + 24]
        for eight in range(4):
            offset = 8 * eight + turn
            if 1 <= offset <= 31:
                yield offset, part[8 * eight : 8 * eight + frames]


def block_kernel(
    n_seq,
    n_dp,
    rows_each,
    score_scale,
    norm_factor,
    len_ref,
    pick_ref,
    kern_ref,
    q_hbm,
    k_hbm,
    v_hbm,
    in_hbm,
    cot_hbm,
    w_hbm,
    conv_ref,
    cgrad_ref,
    sum_ref,
    tile_ref,
    q_ref,
    k_ref,
    v_ref,
    in_ref,
    cot_ref,
    w_ref,
    send,
    recv,
    back,
    home,
    cot_edge,
    hid_edge,
    cot_pad,
    hid_pad,
    hidden,
    grad,
    grad_stack,
    ctx,
    ctx_stack,
    grad_picked,
    kern_grad,
    x_ref,
    parts,
    mine,
    sums,
    whole,
    tile,
    tile_parts,
    tile_mine,
    tile_sums,
    load_sem,
    send_sem,
    recv_sem,
    back_sem,
    home_sem,
    edge_send,
    edge_recv,
    s1,
    r1,
    s2,
    r2,
    s3,
    r3,
    s4,
    r4,
    s5,
    r5,
):
    utts, frames, width = q_ref.shape
    taps = kern_ref.shape[0]
    lanes = PICK_TILE // 128
    held = rows_each * lanes
    reach = 16
    tokens = utts * frames
    block = width // n_seq
    head_size = width // HEADS
    me = lax.axis_index("seq")
    me_dp = lax.axis_index("dp")
    right, left = lax.rem(me + 1, n_seq), lax.rem(me + n_seq - 1, n_seq)
    loads = [
        pltpu.make_async_copy(src, dst, load_sem.at[i])
        for i, (src, dst) in enumerate(
            (
                (cot_hbm, cot_ref),
                (q_hbm, q_ref),
                (k_hbm, k_ref),
                (v_hbm, v_ref),
                (w_hbm, w_ref),
                (in_hbm, in_ref),
            )
        )
    ]
    for load in loads:
        load.start()
    greet((("seq", n_seq), ("dp", n_dp)))

    def swap_edges(rows, edge, utt, base):
        return [
            send_to(
                rows.at[utt, frames - reach : frames],
                edge.at[0, utt],
                edge_send.at[base],
                edge_recv.at[base],
                "seq",
                right,
            ),
            send_to(
                rows.at[utt, 0:reach],
                edge.at[1, utt],
                edge_send.at[base + 1],
                edge_recv.at[base + 1],
                "seq",
                left,
            ),
        ]

    def pad_edges(edge, pad):
        for utt in range(utts):
            before = edge[0, utt].astype(jnp.float32)
            after = edge[1, utt].astype(jnp.float32)
            pad[utt, 0:reach, :] = jnp.where(me > 0, before, 0.0)
            pad[utt, reach + frames : 2 * reach + frames, :] = jnp.where(
                me < n_seq - 1, after, 0.0
            )

    half = frames // 2

    def send_heads(utt):
        for owner in range(n_seq):
            for part in range(2):
                for place, ref in enumerate((q_ref, k_ref, v_ref)):
                    begin = (part * 3 + place) * block
                    send[utt, owner, :, begin : begin + block] = ref[
                        utt, part * half : (part + 1) * half, owner * block : (owner + 1) * block
                    ]
        sent = [
            send_to(
                send.at[utt, peer],
                recv.at[utt, me],
                send_sem.at[utt, i],
                recv_sem.at[utt, i],
                "seq",
                peer,
            )
            for i, peer in enumerate(peers_of("seq", n_seq))
        ]
        recv[utt, pl.ds(me, 1)] = send[utt, pl.ds(me, 1)]
        return sent

    def attend(utt):
        full = n_seq * frames
        key_ok = lax.broadcasted_iota(jnp.int32, (full, full), 1) < len_ref[utt]
        for head in range(block // head_size):
            three = []
            for place in range(3):
                pieces = []
                for part in range(2):
                    begin = (part * 3 + place) * block + head * head_size
                    pieces.append(recv[utt, :, :, begin : begin + head_size])
                three.append(jnp.concatenate(pieces, axis=1).reshape(full, head_size))
            query, key, value = three
            scores = lax.dot_general(
                query, key, (((1,), (1,)), ((), ())), preferred_element_type=jnp.float32
            )
            scores = jnp.where(key_ok, scores * score_scale, neg_big)
            probs = jnp.exp(scores - jnp.max(scores, axis=-1, keepdims=True))
            denom = jnp.sum(probs, axis=-1, keepdims=True)
            rows = jnp.dot(probs.astype(jnp.bfloat16), value, preferred_element_type=jnp.float32)
            rows = (rows / denom).astype(jnp.bfloat16).reshape(n_seq, frames, head_size)
            for part in range(2):
                begin = part * block + head * head_size
                back[utt, :, :, begin : begin + head_size] = rows[
                    :, part * half : (part + 1) * half
                ]
        sent = [
            send_to(
                back.at[utt, peer],
                home.at[utt, me],
                back_sem.at[utt, i],
                home_sem.at[utt, i],
                "seq",
                peer,
            )
            for i, peer in enumerate(peers_of("seq", n_seq))
        ]
        home[utt, pl.ds(me, 1)] = back[utt, pl.ds(me, 1)]
        return sent

    def project(utt):
        first_row = utt * frames
        for owner in range(n_seq):
            for part in range(2):
                rows = slice(first_row + part * half, first_row + (part + 1) * half)
                ctx[rows, owner * block : (owner + 1) * block] = home[
                    utt, owner, :, part * block : (part + 1) * block
                ]
        rows = slice(first_row, first_row + frames)

        @pl.loop(0, width // LOW)
        def _(step):
            cols = pl.ds(pl.multiple_of(step * LOW, LOW), LOW)
            value = jnp.dot(ctx[rows, :], w_ref[:, cols], preferred_element_type=jnp.float32)
            value = in_ref[utt, :, cols].astype(jnp.float32) + value
            value = jnp.where(frame_ids < len_ref[utt], value, 0.0).astype(jnp.bfloat16)
            hidden[utt, :, cols] = value
            hid_pad[utt, reach : reach + frames, cols] = value.astype(jnp.float32)

        sent = swap_edges(hidden, hid_edge, utt, 2 * utts + 2 * utt)
        stack_groups(ctx_stack, ctx[rows, :], first_row, width // LOW)
        return sent

    def pick_context(owner):
        for row in range(rows_each):
            index = lax.div(pick_row(owner, row), width)
            total = jnp.zeros((GROUP, PICK_TILE), jnp.float32)
            for begin, found in choose_groups(ctx_stack[...], tokens, index):
                other = grad_picked[owner, row, begin : begin + GROUP, :]
                total = total + found * other.astype(jnp.float32)
            store_row(x_ref.at[owner], row, jnp.sum(total, axis=0, keepdims=True))

    def kernel_part(step):
        cols = pl.ds(pl.multiple_of(step * 128, 128), 128)
        found = {}
        for utt in range(utts):
            cot = cot_pad[utt, reach : reach + frames, cols]
            for offset, window in shifted_windows(hid_pad[utt, :, cols], frames):
                value = jnp.sum((window * cot).reshape(frames // 8, 8, 128), axis=0)
                found[offset] = value if utt == 0 else found[offset] + value
        for offset, value in found.items():
            kern_grad[offset - 1 : offset, cols] = jnp.sum(value, axis=0, keepdims=True)

    def pick_row(owner, row):
        return jnp.concatenate(
            [pick_ref[owner, lanes * row + i : lanes * row + i + 1, :] for i in range(lanes)],
            axis=1,
        )

    def store_row(ref, row, value):
        for i in range(lanes):
            place = slice(lanes * row + i, lanes * row + i + 1)
            ref[place, :] = value[:, i * 128 : (i + 1) * 128]

    for load in loads[:4]:
        load.wait()
    copies = send_heads(0)
    edges = []
    for utt in range(utts):
        edges += swap_edges(cot_ref, cot_edge, utt, 2 * utt)

    frame_ids = me * frames + lax.broadcasted_iota(jnp.int32, (frames, 1), 0)
    for utt in range(utts):
        cot_pad[utt, reach : reach + frames, :] = cot_ref[utt].astype(jnp.float32)
    for copy in edges:
        copy.wait_recv()
    pad_edges(cot_edge, cot_pad)

    @pl.loop(0, width // 128)
    def _(step):
        cols = pl.ds(pl.multiple_of(step * 128, 128), 128)
        kern = kern_ref[:, cols].astype(jnp.float32)
        for utt in range(utts):
            total = jnp.zeros((frames, 128), jnp.float32)
            for offset, window in shifted_windows(cot_pad[utt, :, cols], frames):
                tap = taps - offset
                total = total + kern[tap : tap + 1] * window
            total = jnp.where(frame_ids < len_ref[utt], total, 0.0)
            grad[utt * frames : (utt + 1) * frames, cols] = total.astype(jnp.bfloat16)

    stack_groups(grad_stack, grad[...], 0, width // LOW)

    def pick_grad(begin, end):
        @pl.loop(begin, end)
        def _(owner):
            for row in range(rows_each):
                index = lax.rem(pick_row(owner, row), width)
                for begin, found in choose_groups(grad_stack[...], tokens, index):
                    grad_picked[owner, row, begin : begin + GROUP, :] = found.astype(jnp.bfloat16)

    for utt in range(1, utts):
        copies += send_heads(utt)
    pick_grad(0, n_seq)
    returns = []
    for utt in range(utts):
        for copy in copies[utt * (n_seq - 1) : (utt + 1) * (n_seq - 1)]:
            copy.wait_recv()
        returns += attend(utt)
    loads[4].wait()
    loads[5].wait()

    @pl.loop(0, width // LOW)
    def _(step):
        cols = pl.ds(pl.multiple_of(step * LOW, LOW), LOW)
        value = lax.dot_general(
            grad[...], w_ref[cols, :], (((1,), (1,)), ((), ())), preferred_element_type=jnp.float32
        ).astype(jnp.bfloat16)
        for row in range(utts):
            cgrad_ref[row, :, cols] = value[row * frames : (row + 1) * frames]

    hid_copies = []
    for utt in range(utts):
        for copy in returns[utt * (n_seq - 1) : (utt + 1) * (n_seq - 1)]:
            copy.wait_recv()
        hid_copies += project(utt)
    kern_grad[...] = jnp.zeros_like(kern_grad)
    alone = n_seq // 2
    rounds = n_seq - alone
    steps = width // 128

    @pl.loop(0, alone)
    def _(owner):
        pick_context(owner)

    for copy in hid_copies:
        copy.wait_recv()
    pad_edges(hid_edge, hid_pad)

    @pl.loop(0, rounds)
    def _(turn):
        pick_context(alone + turn)
        for i in range(steps // rounds):
            kernel_part(turn * (steps // rounds) + i)

    first = [
        send_to(x_ref.at[peer], parts.at[me], s1.at[i], r1.at[i], "seq", peer)
        for i, peer in enumerate(peers_of("seq", n_seq))
    ]
    parts[pl.ds(me, 1)] = x_ref[pl.ds(me, 1)]

    @pl.loop(steps // rounds * rounds, steps)
    def _(step):
        kernel_part(step)

    pick = pick_row(n_seq - 1, rows_each - 1)
    rest = jnp.concatenate(
        [kern_grad[:, part * LOW : (part + 1) * LOW] for part in range(width // LOW)], axis=0
    )
    found = jnp.zeros((kern_grad.shape[0], PICK_TILE), jnp.float32)
    for _ in range(3):
        piece = rest.astype(jnp.bfloat16)
        rest = rest - piece.astype(jnp.float32)
        found = found + choose(piece, kern_grad.shape[0], lax.rem(pick, width))
    tap_ids = lax.broadcasted_iota(jnp.int32, found.shape, 0)
    found = jnp.where(tap_ids == lax.div(pick, width), found, 0.0)
    tile[...] = jnp.zeros_like(tile)
    store_row(tile, 0, jnp.sum(found, axis=0, keepdims=True))

    tile_first = [
        send_to(tile, tile_parts.at[me], s4.at[i], r4.at[i], "seq", peer)
        for i, peer in enumerate(peers_of("seq", n_seq))
    ]
    tile_parts[pl.ds(me, 1)] = tile[...][None]

    def convolve(begin, end):
        @pl.loop(begin, end)
        def _(step):
            cols = pl.ds(pl.multiple_of(step * 128, 128), 128)
            kern = kern_ref[:, cols].astype(jnp.float32)
            for utt in range(utts):
                total = jnp.zeros((frames, 128), jnp.float32)
                for offset, window in shifted_windows(hid_pad[utt, :, cols], frames):
                    total = total + kern[offset - 1 : offset] * window
                conv_ref[utt, :, cols] = total.astype(jnp.bfloat16)

    third_part = width // 128 // 3
    for copy in first:
        copy.wait_recv()
    mine[...] = jnp.sum(parts[...], axis=0)
    second = [
        send_to(mine, sums.at[me_dp], s2.at[i], r2.at[i], "dp", peer)
        for i, peer in enumerate(peers_of("dp", n_dp))
    ]
    sums[pl.ds(me_dp, 1)] = mine[...][None]
    convolve(0, third_part)
    for copy in tile_first:
        copy.wait_recv()
    tile_mine[...] = jnp.sum(tile_parts[...], axis=0)
    tile_second = [
        send_to(tile_mine, tile_sums.at[me_dp], s5.at[i], r5.at[i], "dp", peer)
        for i, peer in enumerate(peers_of("dp", n_dp))
    ]
    tile_sums[pl.ds(me_dp, 1)] = tile_mine[...][None]
    for copy in second:
        copy.wait_recv()
    whole[pl.ds(me, 1)] = (jnp.sum(sums[...], axis=0) * norm_factor)[None]
    third = [
        send_to(whole.at[me], whole.at[me], s3.at[i], r3.at[i], "seq", peer)
        for i, peer in enumerate(peers_of("seq", n_seq))
    ]
    convolve(third_part, width // 128)
    for copy in tile_second:
        copy.wait_recv()
    tile_ref[...] = jnp.sum(tile_sums[...], axis=0)[: tile_ref.shape[0]] * norm_factor
    for copy in third:
        copy.wait_recv()
    for owner in range(n_seq):
        sum_ref[owner * held : (owner + 1) * held] = whole[owner]
    for copy in edges + copies + returns + hid_copies + first + second + third:
        copy.wait_send()
    for copy in tile_first + tile_second:
        copy.wait_send()


def write_kernel(count, *refs):
    sources, outs, held = refs[:count], refs[count : 2 * count], refs[2 * count : 3 * count]
    in_sems, out_sems = refs[3 * count :]
    reads = [pltpu.make_async_copy(sources[i], held[i], in_sems.at[i]) for i in range(count)]
    writes = [pltpu.make_async_copy(held[i], outs[i], out_sems.at[i]) for i in range(count)]
    for copy in reads:
        copy.start()
    for read, write in zip(reads, writes):
        read.wait()
        write.start()
    for copy in writes:
        copy.wait()


def written(*arrays):
    spec = pl.BlockSpec(memory_space=pl.ANY)
    count = len(arrays)
    sems = pltpu.SemaphoreType.DMA((count,))
    return pl.pallas_call(
        functools.partial(write_kernel, count),
        out_shape=[jax.ShapeDtypeStruct(array.shape, array.dtype) for array in arrays],
        in_specs=[spec] * count,
        out_specs=[spec] * count,
        scratch_shapes=[pltpu.VMEM(array.shape, array.dtype) for array in arrays] + [sems, sems],
        compiler_params=pltpu.CompilerParams(vmem_limit_bytes=56 * 2**20),
    )(*arrays)


def one_kernel(
    queries,
    key_rows,
    value_rows,
    layer_input,
    utt_lengths,
    out_weight,
    conv_kernel,
    conv_cotangent,
    pick_weight,
    pick_kernel,
):
    utts, frames, width = queries.shape
    n_seq, n_dp = lax.axis_size("seq"), lax.axis_size("dp")
    block = width // n_seq
    tokens = utts * frames
    tiles = -(-pick_weight.shape[0] // PICK_TILE) + 1
    rows_each = -(-tiles // (2 * n_seq)) * 2
    held_rows = rows_each * PICK_TILE // 128
    kernel_start = (rows_each * n_seq - 1) * PICK_TILE
    picks = jnp.concatenate(
        [
            jnp.pad(pick_weight, (0, kernel_start - pick_weight.shape[0])),
            jnp.pad(pick_kernel, (0, PICK_TILE - pick_kernel.shape[0])),
        ]
    ).reshape(n_seq, held_rows, 128)
    vmem = pl.BlockSpec(memory_space=pltpu.VMEM)
    hbm = pl.BlockSpec(memory_space=pl.ANY)
    bf16, f32 = jnp.bfloat16, jnp.float32
    local = pltpu.VMEM((utts, frames, width), bf16)
    wide = pltpu.VMEM((utts, n_seq, frames // 2, 6 * block), bf16)
    narrow = pltpu.VMEM((utts, n_seq, frames // 2, 2 * block), bf16)
    edge = pltpu.VMEM((2, utts, 16, width), bf16)
    pad = pltpu.VMEM((utts, frames + 32, width), f32)
    flat = pltpu.VMEM((tokens, width), bf16)
    stack = pltpu.VMEM((tokens * width // LOW, LOW), bf16)
    partial = pltpu.VMEM((n_seq, held_rows, 128), f32)
    seq_sems = pltpu.SemaphoreType.DMA((n_seq - 1,))
    dp_sems = pltpu.SemaphoreType.DMA((n_dp - 1,))
    utt_sems = pltpu.SemaphoreType.DMA((utts, n_seq - 1))
    score_scale = 1.0 / math.sqrt(width // HEADS)
    norm_factor = 1.0 / math.sqrt(utts * n_dp * frames * n_seq)
    conv_out, context_grad, total, tile = pl.pallas_call(
        functools.partial(block_kernel, n_seq, n_dp, rows_each, score_scale, norm_factor),
        out_shape=(
            jax.ShapeDtypeStruct(queries.shape, bf16),
            jax.ShapeDtypeStruct(queries.shape, bf16),
            jax.ShapeDtypeStruct((n_seq * held_rows, 128), f32),
            jax.ShapeDtypeStruct((PICK_TILE // 128, 128), f32),
        ),
        in_specs=[pl.BlockSpec(memory_space=pltpu.SMEM), vmem, vmem] + [hbm] * 6,
        out_specs=(vmem, vmem, vmem, vmem),
        scratch_shapes=[
            local,
            local,
            local,
            local,
            local,
            pltpu.VMEM((width, width), bf16),
            wide,
            wide,
            narrow,
            narrow,
            edge,
            edge,
            pad,
            pad,
            local,
            flat,
            stack,
            flat,
            stack,
            pltpu.VMEM((n_seq, rows_each, tokens, PICK_TILE), bf16),
            pltpu.VMEM((32, width), f32),
            partial,
            partial,
            pltpu.VMEM((held_rows, 128), f32),
            pltpu.VMEM((n_dp, held_rows, 128), f32),
            partial,
            pltpu.VMEM((8, 128), f32),
            pltpu.VMEM((n_seq, 8, 128), f32),
            pltpu.VMEM((8, 128), f32),
            pltpu.VMEM((n_dp, 8, 128), f32),
            pltpu.SemaphoreType.DMA((6,)),
            utt_sems,
            utt_sems,
            utt_sems,
            utt_sems,
            pltpu.SemaphoreType.DMA((4 * utts,)),
            pltpu.SemaphoreType.DMA((4 * utts,)),
            seq_sems,
            seq_sems,
            dp_sems,
            dp_sems,
            seq_sems,
            seq_sems,
            seq_sems,
            seq_sems,
            dp_sems,
            dp_sems,
        ],
        compiler_params=pltpu.CompilerParams(
            collective_id=2, has_side_effects=True, vmem_limit_bytes=56 * 2**20
        ),
    )(
        utt_lengths,
        picks,
        conv_kernel,
        queries,
        key_rows,
        value_rows,
        layer_input,
        conv_cotangent,
        out_weight,
    )
    conv_out, context_grad, total, tile = written(conv_out, context_grad, total, tile)
    flat_total = total.reshape(-1)
    weight_picks = flat_total[: pick_weight.shape[0]]
    kernel_picks = tile.reshape(-1)[: pick_kernel.shape[0]]
    return (conv_out, context_grad, weight_picks, kernel_picks)


def on_device(
    queries,
    key_rows,
    value_rows,
    layer_input,
    utt_lengths,
    out_weight,
    conv_kernel,
    conv_cotangent,
    pick_weight,
    pick_kernel,
):
    local_utts, frames_dev, width = queries.shape
    seq_count = lax.axis_size("seq")
    if HEADS % seq_count == 0:
        return one_kernel(
            queries,
            key_rows,
            value_rows,
            layer_input,
            utt_lengths,
            out_weight,
            conv_kernel,
            conv_cotangent,
            pick_weight,
            pick_kernel,
        )
    full_frames = frames_dev * seq_count
    head_size = width // HEADS
    score_scale = 1.0 / math.sqrt(head_size)
    first_frame = lax.axis_index("seq") * frames_dev
    local_ids = first_frame + jnp.arange(frames_dev, dtype=jnp.int32)
    valid_rows = (local_ids[None, :] < utt_lengths[:, None]).astype(jnp.float32)
    context = gathered_attention(queries, key_rows, value_rows, utt_lengths, score_scale)
    context_flat = context.reshape(local_utts * frames_dev, width)
    projected = jnp.dot(context_flat, out_weight, preferred_element_type=jnp.float32).reshape(
        local_utts, frames_dev, width
    )
    hidden = ((layer_input.astype(jnp.float32) + projected) * valid_rows[:, :, None]).astype(
        jnp.bfloat16
    )
    tap_count = conv_kernel.shape[0]
    half_taps = (tap_count - 1) // 2
    kernel_f = conv_kernel.astype(jnp.float32)
    hidden_pad = padded(hidden, (("seq", 1),), half_taps)
    cot_f = conv_cotangent.astype(jnp.float32)
    conv_sum = jnp.zeros((local_utts, frames_dev, width), jnp.float32)
    kernel_rows = []
    for offset in range(tap_count):
        window = hidden_pad[:, offset : offset + frames_dev].astype(jnp.float32)
        conv_sum = conv_sum + kernel_f[offset] * window
        kernel_rows.append(jnp.sum(window * cot_f, axis=(0, 1)))
    conv_out = conv_sum.astype(jnp.bfloat16)
    kernel_grad = jnp.stack(kernel_rows)
    cot_pad = padded(conv_cotangent, (("seq", 1),), half_taps).astype(jnp.float32)
    back_sum = jnp.zeros((local_utts, frames_dev, width), jnp.float32)
    for offset in range(tap_count):
        begin = 2 * half_taps - offset
        back_sum = back_sum + kernel_f[offset] * cot_pad[:, begin : begin + frames_dev]
    hidden_grad = (back_sum * valid_rows[:, :, None]).astype(jnp.bfloat16)
    grad_flat = hidden_grad.reshape(local_utts * frames_dev, width)
    context_grad = lax.dot_general(
        grad_flat, out_weight, (((1,), (1,)), ((), ())), preferred_element_type=jnp.float32
    )
    context_grad = context_grad.reshape(local_utts, frames_dev, width).astype(jnp.bfloat16)
    weight_vals = picked_products(context_flat, grad_flat, pick_weight)
    kernel_vals = pick_entries(kernel_grad, pick_kernel)
    total = summed(jnp.concatenate([weight_vals, kernel_vals]))
    weight_sum = total[: pick_weight.shape[0]]
    kernel_sum = total[weight_vals.shape[0] : weight_vals.shape[0] + pick_kernel.shape[0]]
    total_slots = local_utts * lax.axis_size("dp") * full_frames
    norm_factor = 1.0 / math.sqrt(total_slots)
    return (conv_out, context_grad, weight_sum * norm_factor, kernel_sum * norm_factor)


def solution(mesh):
    placed = (
        P("dp", "seq", None),
        P("dp", "seq", None),
        P("dp", "seq", None),
        P("dp", "seq", None),
        P("dp"),
        P(),
        P(),
        P("dp", "seq", None),
        P(),
        P(),
    )
    return jax.shard_map(
        on_device,
        mesh=mesh,
        in_specs=placed,
        out_specs=(P("dp", "seq", None), P("dp", "seq", None), P(), P()),
        check_vma=False,
    )
```
